128 devices in a mesh: gx: 32 (over x, y_lo, z), gy: 2 (over y_hi), mode: 2 (over core).
Axes of the slice: x: 4, y: 4 (y_hi: 2, y_lo: 2; y = y_hi * 2 + y_lo), z: 4, core: 2. Of those that a mesh axis runs over, the one named last changes fastest.
Arguments:
- chaos_state: float32 [64, 48, 4, 8192], P('gx', 'mode', None, 'gy'), may hold values from -2.5 to 2.5
- mode_group: int32 [35], replicated, may hold values from 0 to 1, as said below
- mode_degrees: int32 [35, 4], replicated, may hold values from 0 to 3, as said below
Outputs:
- new_state: float32 [64, 48, 4, 8192], P('gx', 'mode', None, 'gy')
The draws below stay inside these ranges and needn't reach their ends.
Inputs may be any that keep to these rules, and one draw needn't show every extreme that they name: mode_group[m] is the group of chaos mode m; every group holds at most 24 modes, and one group holds exactly 24. `mode_degrees`: the rows are the 35 multi-indices of 4 non-negative degrees with sum at most 3, each once, in some order.
All inputs are finite; a program needn't handle non-finite values.
Results may differ from the reference program's by a relative error of at most 0.00005.
Values sent between devices are 32-bit elements; how exact they have to be, the bound alone decides.
No kernel may reach another device: no remote copies, remote signals or barrier semaphores. Data moves between devices by JAX's collectives and lax.ppermute only.
A program may use at most 512 MiB of HBM per device.

```python
import math
import jax
import jax.numpy as jnp
import numpy as np
from jax import lax

FIELDS = 4
PARAMS = 4
MODES = 35
QUAD = 81
NZ = 16
SLOTS = 24
NX = 64
NY = 512
SLOT_ALL = 48
N_MODE = 2


def degree_rows():
    collected = []
    for first_power in range(4):
        for second_power in range(4):
            for third_power in range(4):
                for fourth_power in range(4):
                    if first_power + second_power + third_power + fourth_power <= 3:
                        collected.append([first_power, second_power, third_power, fourth_power])
    return np.array(collected, dtype=np.int32)


def draw_mode_group(key, part):
    key = jax.random.fold_in(key, 11)
    order_key, pick_key = jax.random.split(key)
    shuffled = jax.random.permutation(order_key, MODES).astype(jnp.int32)
    largest = jax.random.randint(pick_key, (), 0, N_MODE, dtype=jnp.int32)
    spread = 1 + (shuffled - SLOTS) % max(N_MODE - 1, 1)
    return jnp.where(shuffled < SLOTS, largest, (largest + spread) % N_MODE).astype(jnp.int32)


def draw_mode_degrees(key, part):
    key = jax.random.fold_in(key, 23)
    degree_table = jnp.asarray(degree_rows(), dtype=jnp.int32)
    return degree_table[jax.random.permutation(key, MODES)]


def block_scale(key, dims, cuts, smallest, high):
    factor_of, own = 1.0, jax.random.fold_in(key, 6)
    for position, blocks in cuts:
        draws = jnp.exp(jax.random.uniform(jax.random.fold_in(own, position), (blocks,), jnp.float32, smallest / len(cuts), high / len(cuts)))
        factor_of = factor_of * jnp.repeat(draws, dims[position] // blocks).reshape([-1 if axis == position else 1 for axis in range(len(dims))])
    return factor_of


def normal_values(own_key, shape, width, bound, cuts=(), kind=jnp.bfloat16):
    values = jax.random.normal(own_key, shape, jnp.float32) * width
    if len(cuts) > 0:
        values = block_scale(own_key, shape, cuts, -0.22, 0.18) * values
    return jnp.clip(values, min=-bound, max=bound).astype(kind)


def setup_inputs(seed: int = 0) -> dict:
    key_of = jax.random.split(jax.random.key(seed), 4)
    chaos_state = normal_values(key_of[0], (NX, SLOT_ALL, FIELDS, NY * NZ), 0.4, 2.5, ((0, 32), (1, 2), (3, 2)), jnp.float32)
    mode_group = draw_mode_group(jax.random.fold_in(key_of[3], 71), 0)
    mode_degrees = draw_mode_degrees(jax.random.fold_in(key_of[3], 71), 0)
    return {"chaos_state": chaos_state, "mode_group": mode_group, "mode_degrees": mode_degrees}


top_degree = lax.Precision.HIGHEST
time_step = 0.05
diffusion = 1.0

def chaos_tables(mode_degrees):
    points = jnp.arange(QUAD, dtype=jnp.int32)
    powers = jnp.power(3, jnp.arange(PARAMS, dtype=jnp.int32)).astype(jnp.int32)
    digits = points[:, None] // powers[None, :] % 3
    abscissa = (digits - 1).astype(jnp.float32) * math.sqrt(3.0)
    weights = jnp.prod(jnp.where(digits == 1, 2.0 / 3.0, 1.0 / 6.0).astype(jnp.float32), axis=1)
    degree = mode_degrees[None, :, :]
    coordinate = abscissa[:, None, :]
    square_term = (coordinate * coordinate - 1.0) / math.sqrt(2.0)
    cubic_term = (coordinate * coordinate * coordinate - 3.0 * coordinate) / math.sqrt(6.0)
    factor = jnp.where(degree == 0, jnp.ones_like(coordinate), jnp.where(degree == 1, coordinate, jnp.where(degree == 2, square_term, cubic_term)))
    chaos_basis_table = jnp.prod(factor, axis=2)
    return (abscissa, weights, chaos_basis_table)

def slot_index(mode_group, slots):
    mode_count = mode_group.shape[0]
    mode_order = jnp.arange(mode_count, dtype=jnp.int32)
    same_group = mode_group[:, None] == mode_group[None, :]
    before = mode_order[None, :] < mode_order[:, None]
    rank_in_group = lax.optimization_barrier(jnp.sum(jnp.where(same_group & before, 1, 0).astype(jnp.int32), axis=1))
    return (mode_group * slots + rank_in_group).astype(jnp.int32)

def point_terms(point_values, abscissa):
    param_one = abscissa[:, 0][:, None, None]
    param_two = abscissa[:, 1][:, None, None]
    param_three = abscissa[:, 2][:, None, None]
    param_four = abscissa[:, 3][:, None, None]
    lead_field = point_values[:, 0:1, :]
    side_field = point_values[:, 1:2, :]
    speed_east = 0.6 + 0.25 * param_one + 0.5 * lead_field
    speed_north = 0.3 + 0.25 * param_two + 0.5 * side_field
    relaxation = 0.4 * jnp.exp(0.25 * param_three)
    coupling = 0.15 * (1.0 + 0.3 * param_four)
    eastward_flux = speed_east * point_values
    northward_flux = speed_north * point_values
    source_term = -relaxation * point_values + coupling * jnp.roll(point_values, -1, axis=1) * jnp.roll(point_values, -2, axis=1)
    return (eastward_flux, northward_flux, source_term)

def centered(plus_one, minus_one, plus_two, minus_two):
    return (8.0 * (plus_one - minus_one) - (plus_two - minus_two)) / 12.0

def plane_laplace(field_array):
    plane_index = jnp.arange(field_array.shape[-1], dtype=jnp.int32) % NZ
    above_plane = jnp.where(plane_index == NZ - 1, jnp.roll(field_array, NZ - 1, axis=-1), jnp.roll(field_array, -1, axis=-1))
    below_plane = jnp.where(plane_index == 0, jnp.roll(field_array, 1 - NZ, axis=-1), jnp.roll(field_array, 1, axis=-1))
    return above_plane - 2.0 * field_array + below_plane

def reference(chaos_state, mode_group, mode_degrees):
    abscissa, weights, chaos_basis_table = chaos_tables(mode_degrees)
    galerkin_projection = jnp.transpose(chaos_basis_table * weights[:, None])
    slot_of_mode = slot_index(mode_group, SLOTS)
    coefficients = jnp.take(chaos_state, slot_of_mode, axis=1)

    def tendency(modal):

        def row_work(row_coefficients):
            point_values = jnp.einsum('as,snj->anj', chaos_basis_table, row_coefficients, precision=top_degree)
            eastward_flux, northward_flux, source_term = point_terms(point_values, abscissa)
            eastward_modal_flux = jnp.einsum('ok,kta->ota', galerkin_projection, eastward_flux, precision=top_degree)
            northward_modal_flux = jnp.einsum('ok,kta->ota', galerkin_projection, northward_flux, precision=top_degree)
            source_modal_terms = jnp.einsum('ok,kta->ota', galerkin_projection, source_term, precision=top_degree)
            north_term = centered(jnp.roll(northward_modal_flux, -NZ, axis=-1), jnp.roll(northward_modal_flux, NZ, axis=-1), jnp.roll(northward_modal_flux, -2 * NZ, axis=-1), jnp.roll(northward_modal_flux, 2 * NZ, axis=-1))
            partial_value = source_modal_terms - north_term + diffusion * plane_laplace(row_coefficients)
            return (eastward_modal_flux, partial_value)
        eastward_modal_flux, partial_value = lax.map(row_work, modal)
        east_term = centered(jnp.roll(eastward_modal_flux, -1, axis=0), jnp.roll(eastward_modal_flux, 1, axis=0), jnp.roll(eastward_modal_flux, -2, axis=0), jnp.roll(eastward_modal_flux, 2, axis=0))
        return partial_value - east_term
    section = coefficients + time_step * tendency(coefficients)
    advanced = 0.5 * coefficients + 0.5 * (section + time_step * tendency(section))
    return jnp.zeros_like(chaos_state).at[:, slot_of_mode].set(advanced)
```

```python
import math

import jax
import jax.numpy as jnp
import numpy as np
from jax import lax
from jax.experimental import pallas as pl
from jax.experimental.pallas import tpu as pltpu
from jax.sharding import Mesh, PartitionSpec as P

MODES = 35
FIELDS = 4
QUAD = 81
POINTS = 96
NZ = 16
SLOTS = 24
SMALL = 16
ROWS = SLOTS + SMALL
LANES = 256
STRIP = 2 * NZ
XROWS = 16
STEP = 4
time_step = 0.05
VMEM = 56 * 1024 * 1024
F32, BF16 = jnp.float32, jnp.bfloat16


def point_constants():
    p = np.arange(POINTS)
    live = (p < QUAD).astype(np.float64)
    digits = [(p // 3**k) % 3 - 1.0 for k in range(4)]
    xi = [math.sqrt(3.0) * d for d in digits]
    weight = live * np.prod([np.where(d == 0, 4.0, 1.0) for d in digits], axis=0)
    east = 1.2 + 0.5 * xi[0]
    north = 0.6 + 0.5 * xi[1]
    decay = -9.6 * np.exp(0.25 * xi[2])
    rows = np.stack(digits + [weight, east, north, decay]).astype(np.float32)
    cols = np.zeros((POINTS, 8), np.float32)
    cols[:, :4] = np.stack(digits, 1)
    cols[:, 4] = live
    return np.concatenate([rows, rows], axis=1), cols


def degree_factor(n, d):
    square = 3.0 * d * d - 1.0
    cubic = d * d * d - d
    return jnp.where(n == 0.0, 1.0, jnp.where(n == 1.0, d, jnp.where(n == 2.0, square, cubic)))


def degree_norm(n):
    third = 3.0 * math.sqrt(3.0) / math.sqrt(6.0)
    return jnp.where(n == 0.0, 1.0, jnp.where(n == 1.0, math.sqrt(3.0), jnp.where(n == 2.0, 1.0 / math.sqrt(2.0), third)))


def table_kernel(grow_ref, gcol_ref, degrees_ref, degrees_t_ref, prow_ref, pcol_ref, eval_ref, proj_ref, scale_ref):
    grow, gcol = grow_ref[...], gcol_ref[...]
    same = gcol == grow
    sub = lax.broadcasted_iota(jnp.int32, (MODES, MODES), 0)
    lane = lax.broadcasted_iota(jnp.int32, (MODES, MODES), 1)
    rank_row = jnp.sum(jnp.where(same & (sub < lane), 1.0, 0.0), axis=0, keepdims=True)
    rank_col = jnp.sum(jnp.where(same & (lane < sub), 1.0, 0.0), axis=1, keepdims=True)
    ones = jnp.sum(grow, axis=1, keepdims=True)
    big = jnp.where(ones == float(SLOTS), 1.0, 0.0)
    place_row = jnp.where(grow == big, rank_row, rank_row + SLOTS)
    place_col = jnp.where(gcol == big, rank_col, rank_col + SLOTS)
    row_id = lax.broadcasted_iota(jnp.int32, (ROWS, MODES), 0).astype(F32)
    pick = jnp.where(row_id == place_row, 1.0, 0.0)
    live_col = jnp.sum(pick, axis=1, keepdims=True)
    degree_col = [jnp.sum(pick * degrees_t_ref[k : k + 1, :], axis=1, keepdims=True) for k in range(4)]
    lane_id = lax.broadcasted_iota(jnp.int32, (MODES, 128), 1)
    lane_row = jnp.where(lane_id < ROWS, lane_id, jnp.where(lane_id < 2 * ROWS, lane_id - ROWS, lane_id - 2 * ROWS)).astype(F32)
    pick_t = jnp.where(lane_row == place_col, 1.0, 0.0)
    live_row = jnp.sum(pick_t, axis=0, keepdims=True)
    degree_row = [jnp.sum(pick_t * degrees_ref[:, k : k + 1], axis=0, keepdims=True) for k in range(4)]
    basis = live_row * pcol_ref[:, 4:5]
    for k in range(4):
        basis = basis * degree_factor(degree_row[k], pcol_ref[:, k : k + 1])
    projector = live_col * prow_ref[4:5, :]
    scale, inverse = live_col, live_col
    for k in range(4):
        projector = projector * degree_factor(degree_col[k], prow_ref[k : k + 1, :])
        norm = degree_norm(degree_col[k])
        scale = scale * norm
        inverse = inverse / norm
    column = lax.broadcasted_iota(jnp.int32, (1, 128), 1)
    eval_ref[0:POINTS, :] = jnp.where(column < 2 * ROWS, basis, 0.0).astype(BF16)
    linear = []
    for k in range(3):
        left = projector[:, :POINTS] * prow_ref[5 + k : 6 + k, :POINTS]
        full = jnp.dot(left, basis, precision=lax.Precision.HIGHEST, preferred_element_type=F32)
        first = full.astype(BF16).astype(F32)
        linear.append(jnp.where(column < 2 * ROWS, first, jnp.where(column < 3 * ROWS, full - first, 0.0)))
    linear.append(jnp.zeros((8, 128), F32))
    eval_ref[POINTS:, :] = jnp.concatenate(linear, axis=0).astype(BF16)
    proj_ref[...] = jnp.concatenate([projector, projector * prow_ref[3:4, :]], axis=0).astype(BF16)
    scale_ref[0] = jnp.broadcast_to(scale, (ROWS, LANES))
    scale_ref[1] = jnp.broadcast_to(scale * scale * (time_step / (24.0 * 1296.0)), (ROWS, LANES))
    scale_ref[2] = jnp.broadcast_to(inverse, (ROWS, LANES))


def make_tables(mode_group, mode_degrees):
    prow, pcol = point_constants()
    group = mode_group.astype(F32)
    degrees = mode_degrees.astype(F32)
    return pl.pallas_call(
        table_kernel,
        out_shape=[
            jax.ShapeDtypeStruct((POINTS + 128, 128), BF16),
            jax.ShapeDtypeStruct((2 * ROWS, 2 * POINTS), BF16),
            jax.ShapeDtypeStruct((3, ROWS, LANES), F32),
        ],
        name="tables",
    )(group[None, :], group[:, None], degrees, degrees.T, jnp.asarray(prow), jnp.asarray(pcol))


def lane_index():
    return lax.broadcasted_iota(jnp.int32, (1, LANES), 1)


def shift_masks():
    lane = lane_index()
    return [
        jnp.where(lane < LANES - NZ, 8.0, 0.0),
        jnp.where(lane >= NZ, 8.0, 0.0),
        jnp.where(lane < LANES - 2 * NZ, 1.0, 0.0),
        jnp.where(lane >= 2 * NZ, 1.0, 0.0),
    ]


def rolled(value, shift):
    return pltpu.roll(value, shift % value.shape[1], 1)


def difference_y(value):
    up, down, up_two, down_two = shift_masks()
    return (up * rolled(value, -NZ) - down * rolled(value, NZ)) - (up_two * rolled(value, -2 * NZ) - down_two * rolled(value, 2 * NZ))


def plane_laplace(value):
    plane = lane_index() % NZ
    above = jnp.where(plane == NZ - 1, rolled(value, NZ - 1), rolled(value, -1))
    below = jnp.where(plane == 0, rolled(value, 1 - NZ), rolled(value, 1))
    return above - 2.0 * value + below


def row_fluxes(fields, eval_ref, proj_ref):
    points, east, north, source = [], [], [], []
    for value in fields:
        first = value.astype(BF16).astype(F32)
        stack = jnp.concatenate([first, value - first, first, jnp.zeros((8, LANES), F32)], axis=0).astype(BF16)
        result = jnp.dot(eval_ref[...], stack, preferred_element_type=F32)
        points.append(result[0:POINTS])
        east.append(result[POINTS : POINTS + ROWS])
        north.append(result[POINTS + ROWS : POINTS + 2 * ROWS])
        source.append(result[POINTS + 2 * ROWS : POINTS + 3 * ROWS])

    def project(a, b, both):
        product = points[a] * points[b]
        first = product.astype(BF16)
        second = (product - first.astype(F32)).astype(BF16)
        stack = jnp.concatenate([first, second], axis=0)
        left = proj_ref[...] if both else proj_ref[0:48, :]
        return jnp.dot(left, stack, preferred_element_type=F32)

    def couple(f, result):
        source[f] = source[f] + (3.6 * result[0:ROWS] + (1.08 * math.sqrt(3.0)) * result[ROWS : 2 * ROWS])

    east[0] = east[0] + project(0, 0, False)[0:ROWS]
    result = project(0, 1, True)
    east[1] = east[1] + result[0:ROWS]
    north[0] = north[0] + result[0:ROWS]
    couple(3, result)
    east[2] = east[2] + project(0, 2, False)[0:ROWS]
    result = project(0, 3, True)
    east[3] = east[3] + result[0:ROWS]
    couple(2, result)
    north[1] = north[1] + project(1, 1, False)[0:ROWS]
    result = project(1, 2, True)
    north[2] = north[2] + result[0:ROWS]
    couple(0, result)
    north[3] = north[3] + project(1, 3, False)[0:ROWS]
    couple(1, project(2, 3, True))
    return east, north, source


def emit_row(r, fields, base, weight, eval_ref, proj_ref, scale_ref, east_ref, next_ref, low_ref, high_ref):
    east, north, source = row_fluxes(fields, eval_ref, proj_ref)
    gain = scale_ref[1]
    lane = lax.broadcasted_iota(jnp.int32, (1, 128), 1)
    here = (lane >= r * STRIP) & (lane < (r + 1) * STRIP)
    for f in range(FIELDS):
        rows = slice(f * ROWS, (f + 1) * ROWS)
        east_ref[r, rows, :] = east[f]
        known = gain * (source[f] - difference_y(north[f])) + time_step * plane_laplace(fields[f])
        next_ref[r, rows, :] = base[f] + weight * known
        low = pltpu.roll(north[f][:, :128], r * STRIP, 1)
        high = pltpu.roll(north[f][:, 128:], (r * STRIP + STRIP) % 128, 1)
        if r == 0:
            low_ref[0, rows, :] = low
            high_ref[0, rows, :] = high
        else:
            low_ref[0, rows, :] = jnp.where(here, low, low_ref[0, rows, :])
            high_ref[0, rows, :] = jnp.where(here, high, high_ref[0, rows, :])


def from_neighbours(r, f, centre, before_ref, after_ref, low_ref, high_ref, first, last, edge_before, edge_after):
    rows = slice(f * ROWS, (f + 1) * ROWS)

    def row(k):
        if k < 0:
            return jnp.where(first, edge_before[k + 2, rows, :], before_ref[k + 2, rows, :])
        if k >= STEP:
            return jnp.where(last, edge_after[k - STEP, rows, :], after_ref[k - STEP, rows, :])
        return centre[k, rows, :]

    total = 8.0 * (row(r + 1) - row(r - 1)) - (row(r + 2) - row(r - 2))
    lane = lax.broadcasted_iota(jnp.int32, (1, 128), 1)
    below = pltpu.roll(high_ref[0, rows, :], (128 - r * STRIP) % 128, 1)
    above = pltpu.roll(low_ref[0, rows, :], (96 - r * STRIP) % 128, 1)
    low = jnp.where(lane < STRIP, below, 0.0) - jnp.where(lane < NZ, 8.0, 0.0) * pltpu.roll(below, 128 - NZ, 1)
    high = jnp.where(lane >= 128 - NZ, 8.0, 0.0) * pltpu.roll(above, NZ, 1) - jnp.where(lane >= 128 - STRIP, above, 0.0)
    return total + jnp.concatenate([low, high], axis=1)


def first_kernel(big_ref, state_ref, eval_ref, proj_ref, scale_ref, coef_ref, east_ref, next_ref, low_ref, high_ref):
    big = big_ref[0]
    for r in range(STEP):
        chip, x = divmod(r, 2)
        fields = []
        for f in range(FIELDS):
            halves = []
            for half in range(2):
                full = state_ref[2 * chip + big, x, half, pl.ds(f, SLOTS, stride=FIELDS), :]
                rest = state_ref[2 * chip + 1 - big, x, half, pl.ds(f, SMALL, stride=FIELDS), :]
                halves.append(jnp.concatenate([full, rest], axis=0))
            value = scale_ref[0] * jnp.concatenate(halves, axis=1)
            coef_ref[r, f * ROWS : (f + 1) * ROWS, :] = value
            fields.append(value)
        emit_row(r, fields, fields, 1.0, eval_ref, proj_ref, scale_ref, east_ref, next_ref, low_ref, high_ref)


def middle_kernel(coef_ref, next_ref, east_ref, before_ref, after_ref, low_ref, high_ref, edge_before, edge_after, eval_ref, proj_ref, scale_ref, east_out, next_out, low_out, high_out):
    first = pl.program_id(0) == 0
    last = pl.program_id(0) == pl.num_programs(0) - 1
    for r in range(STEP):
        section, base = [], []
        for f in range(FIELDS):
            rows = slice(f * ROWS, (f + 1) * ROWS)
            missing = from_neighbours(r, f, east_ref, before_ref, after_ref, low_ref, high_ref, first, last, edge_before, edge_after)
            section.append(next_ref[r, rows, :] - scale_ref[1] * missing)
            base.append(0.5 * (coef_ref[r, rows, :] + section[f]))
        emit_row(r, section, base, 0.5, eval_ref, proj_ref, scale_ref, east_out, next_out, low_out, high_out)


def last_kernel(big_ref, next_ref, east_ref, before_ref, after_ref, low_ref, high_ref, edge_before, edge_after, scale_ref, state_out):
    big = big_ref[0]
    first = pl.program_id(0) == 0
    last = pl.program_id(0) == pl.num_programs(0) - 1
    for r in range(STEP):
        chip, x = divmod(r, 2)
        for f in range(FIELDS):
            rows = slice(f * ROWS, (f + 1) * ROWS)
            missing = from_neighbours(r, f, east_ref, before_ref, after_ref, low_ref, high_ref, first, last, edge_before, edge_after)
            value = scale_ref[2] * (next_ref[r, rows, :] - 0.5 * scale_ref[1] * missing)
            rest = jnp.concatenate([value[SLOTS:], jnp.zeros((SLOTS - SMALL, LANES), F32)], axis=0)
            for half in range(2):
                lanes = slice(half * 128, (half + 1) * 128)
                state_out[2 * chip + big, x, half, pl.ds(f, SLOTS, stride=FIELDS), :] = value[:SLOTS, lanes]
                state_out[2 * chip + 1 - big, x, half, pl.ds(f, SLOTS, stride=FIELDS), :] = rest[:, lanes]


def whole(shape):
    return pl.BlockSpec(shape, lambda i: (0,) * len(shape))


def kernels():
    steps = XROWS // STEP
    tall = FIELDS * ROWS
    smem = pl.BlockSpec(memory_space=pltpu.SMEM)
    rows = pl.BlockSpec((STEP, tall, LANES), lambda i: (i, 0, 0))
    before = pl.BlockSpec((2, tall, LANES), lambda i: (jnp.maximum(2 * i - 1, 0), 0, 0))
    after = pl.BlockSpec((2, tall, LANES), lambda i: (jnp.minimum(2 * i + 2, 2 * steps - 1), 0, 0))
    strip = pl.BlockSpec((1, tall, 128), lambda i: (i, 0, 0))
    edge = whole((2, tall, LANES))
    state = pl.BlockSpec((STEP, 2, 2, SLOTS * FIELDS, 128), lambda i: (i, 0, 0, 0, 0))
    evaluate, proj, scale = whole((POINTS + 128, 128)), whole((2 * ROWS, 2 * POINTS)), whole((3, ROWS, LANES))
    rows_shape = jax.ShapeDtypeStruct((XROWS, tall, LANES), F32)
    strip_shape = jax.ShapeDtypeStruct((steps, tall, 128), F32)
    state_shape = jax.ShapeDtypeStruct((16, 2, 2, SLOTS * FIELDS, 128), F32)
    params = pltpu.CompilerParams(vmem_limit_bytes=VMEM, dimension_semantics=("arbitrary",))
    neighbours = [rows, before, after, strip, strip, edge, edge]
    first = pl.pallas_call(
        first_kernel,
        grid=(steps,),
        in_specs=[smem, state, evaluate, proj, scale],
        out_specs=[rows, rows, rows, strip, strip],
        out_shape=[rows_shape, rows_shape, rows_shape, strip_shape, strip_shape],
        compiler_params=params,
        name="first_section",
    )
    middle = pl.pallas_call(
        middle_kernel,
        grid=(steps,),
        in_specs=[rows, rows] + neighbours + [evaluate, proj, scale],
        out_specs=[rows, rows, strip, strip],
        out_shape=[rows_shape, rows_shape, strip_shape, strip_shape],
        compiler_params=params,
        name="second_section",
    )
    final = pl.pallas_call(
        last_kernel,
        grid=(steps,),
        in_specs=[smem, rows] + neighbours + [scale],
        out_specs=state,
        out_shape=state_shape,
        compiler_params=params,
        name="advanced",
    )
    return first, middle, final


def ring(size, step):
    return [(i, (i + step) % size) for i in range(size)]


def exchange(east, low, high):
    before = lax.ppermute(east[XROWS - 2 :], "gx_hi", ring(lax.axis_size("gx_hi"), 1))
    after = lax.ppermute(east[:2], "gx_hi", ring(lax.axis_size("gx_hi"), -1))
    axes = ("gx_lo", "gy", "mode")
    place = [(chip * 2 + side) * 2 + core for side in range(2) for chip in range(8) for core in range(2)]
    up = [(place[i], place[(i + 1) % 32]) for i in range(32)]
    below = lax.ppermute(high, axes, up)
    above = lax.ppermute(low, axes, [(b, a) for a, b in up])
    return above, below, before, after


def shards(chaos_state, mode_group, mode_degrees):
    big = jnp.where(jnp.sum(mode_group) == SLOTS, 1, 0).astype(jnp.int32).reshape(1)
    evaluate, proj, scale = make_tables(mode_group, mode_degrees)
    first, middle, final = kernels()
    blocks = chaos_state.reshape(2, SLOTS, FIELDS, 16, 2, 128).transpose(3, 0, 4, 1, 2, 5)
    blocks = blocks.reshape(16, 2, 2, SLOTS * FIELDS, 128)
    tile = lax.all_to_all(blocks, ("gx_lo", "mode"), 0, 0, tiled=True)
    coef, east, following, low, high = first(big, tile, evaluate, proj, scale)
    above, below, before, after = exchange(east, low, high)
    east, following, low, high = middle(coef, following, east, east, east, above, below, before, after, evaluate, proj, scale)
    above, below, before, after = exchange(east, low, high)
    tile = final(big, following, east, east, east, above, below, before, after, scale)
    blocks = lax.all_to_all(tile, ("gx_lo", "mode"), 0, 0, tiled=True)
    blocks = blocks.reshape(16, 2, 2, SLOTS, FIELDS, 128).transpose(1, 3, 4, 0, 2, 5)
    return blocks.reshape(2, SLOTS, FIELDS, 16 * LANES)


def solution(mesh):
    fine = Mesh(mesh.devices.reshape(4, 8, 2, 2), ("gx_hi", "gx_lo", "gy", "mode"))
    spec = P(("gx_hi", "gx_lo"), "mode", None, "gy")
    return jax.shard_map(shards, mesh=fine, in_specs=(spec, P(), P()), out_specs=spec, check_vma=False)
```

```python
import math

import jax
import jax.numpy as jnp
import numpy as np
from jax import lax
from jax.experimental import pallas as pl
from jax.experimental.pallas import tpu as pltpu
from jax.sharding import Mesh, PartitionSpec as P

MODES = 35
FIELDS = 4
QUAD = 81
POINTS = 96
NZ = 16
SLOTS = 24
REST = MODES - SLOTS
SMALL = 16
PIECE = 2 * MODES * FIELDS
FULL_AT = 2 * REST * FIELDS
ROWS = SLOTS + SMALL
LANES = 256
STRIP = 2 * NZ
XROWS = 16
STEP = 4
time_step = 0.05
LIMIT = 40 * 1024 * 1024
F32, BF16 = jnp.float32, jnp.bfloat16


def point_constants():
    p = np.arange(POINTS)
    live = (p < QUAD).astype(np.float64)
    digits = [(p // 3**k) % 3 - 1.0 for k in range(4)]
    xi = [math.sqrt(3.0) * d for d in digits]
    weight = live * np.prod([np.where(d == 0, 4.0, 1.0) for d in digits], axis=0)
    east = 1.2 + 0.5 * xi[0]
    north = 0.6 + 0.5 * xi[1]
    decay = -9.6 * np.exp(0.25 * xi[2])
    rows = np.stack(digits + [weight, east, north, decay]).astype(np.float32)
    cols = np.zeros((POINTS, 8), np.float32)
    cols[:, :4] = np.stack(digits, 1)
    cols[:, 4] = live
    return np.concatenate([rows, rows], axis=1), cols


def degree_factor(n, d):
    square = 3.0 * d * d - 1.0
    cubic = d * d * d - d
    return jnp.where(n == 0.0, 1.0, jnp.where(n == 1.0, d, jnp.where(n == 2.0, square, cubic)))


def degree_norm(n):
    third = 3.0 * math.sqrt(3.0) / math.sqrt(6.0)
    return jnp.where(n == 0.0, 1.0, jnp.where(n == 1.0, math.sqrt(3.0), jnp.where(n == 2.0, 1.0 / math.sqrt(2.0), third)))


def table_kernel(group_ref, degrees_ref, prow_ref, pcol_ref, eval_ref, proj_ref, scale_ref, big_ref):
    sub = lax.broadcasted_iota(jnp.int32, (MODES, MODES), 0)
    lane = lax.broadcasted_iota(jnp.int32, (MODES, MODES), 1)
    grow = group_ref[...].astype(F32)
    gcol = jnp.sum(jnp.where(sub == lane, grow, 0.0), axis=1, keepdims=True)
    degrees = degrees_ref[...].astype(F32)
    degrees_t = [jnp.sum(jnp.where(sub == lane, degrees[:, k : k + 1], 0.0), axis=0, keepdims=True) for k in range(4)]
    big_ref[0] = jnp.where(jnp.sum(grow) == float(SLOTS), 1, 0).astype(jnp.int32)
    same = gcol == grow
    rank_row = jnp.sum(jnp.where(same & (sub < lane), 1.0, 0.0), axis=0, keepdims=True)
    rank_col = jnp.sum(jnp.where(same & (lane < sub), 1.0, 0.0), axis=1, keepdims=True)
    ones = jnp.sum(grow, axis=1, keepdims=True)
    big = jnp.where(ones == float(SLOTS), 1.0, 0.0)
    place_row = jnp.where(grow == big, rank_row, rank_row + SLOTS)
    place_col = jnp.where(gcol == big, rank_col, rank_col + SLOTS)
    row_id = lax.broadcasted_iota(jnp.int32, (ROWS, MODES), 0).astype(F32)
    pick = jnp.where(row_id == place_row, 1.0, 0.0)
    live_col = jnp.sum(pick, axis=1, keepdims=True)
    degree_col = [jnp.sum(pick * degrees_t[k], axis=1, keepdims=True) for k in range(4)]
    lane_id = lax.broadcasted_iota(jnp.int32, (MODES, 128), 1)
    lane_row = jnp.where(lane_id < ROWS, lane_id, jnp.where(lane_id < 2 * ROWS, lane_id - ROWS, lane_id - 2 * ROWS)).astype(F32)
    pick_t = jnp.where(lane_row == place_col, 1.0, 0.0)
    live_row = jnp.sum(pick_t, axis=0, keepdims=True)
    degree_row = [jnp.sum(pick_t * degrees[:, k : k + 1], axis=0, keepdims=True) for k in range(4)]
    basis = live_row * pcol_ref[:, 4:5]
    for k in range(4):
        basis = basis * degree_factor(degree_row[k], pcol_ref[:, k : k + 1])
    projector = live_col * prow_ref[4:5, :]
    scale, inverse = live_col, live_col
    for k in range(4):
        projector = projector * degree_factor(degree_col[k], prow_ref[k : k + 1, :])
        norm = degree_norm(degree_col[k])
        scale = scale * norm
        inverse = inverse / norm
    column = lax.broadcasted_iota(jnp.int32, (1, 128), 1)
    eval_ref[0:POINTS, :] = jnp.where(column < 2 * ROWS, basis, 0.0).astype(BF16)
    linear = []
    for k in range(3):
        left = projector[:, :POINTS] * prow_ref[5 + k : 6 + k, :POINTS]
        full = jnp.dot(left, basis, precision=lax.Precision.HIGHEST, preferred_element_type=F32)
        first = full.astype(BF16).astype(F32)
        linear.append(jnp.where(column < 2 * ROWS, first, jnp.where(column < 3 * ROWS, full - first, 0.0)))
    linear.append(jnp.zeros((8, 128), F32))
    eval_ref[POINTS:, :] = jnp.concatenate(linear, axis=0).astype(BF16)
    proj_ref[...] = jnp.concatenate([projector, projector * prow_ref[3:4, :]], axis=0).astype(BF16)
    scale_ref[0] = jnp.broadcast_to(scale, (ROWS, LANES))
    scale_ref[1] = jnp.broadcast_to(scale * scale * (time_step / (24.0 * 1296.0)), (ROWS, LANES))
    scale_ref[2] = jnp.broadcast_to(inverse, (ROWS, LANES))


def make_tables(mode_group, mode_degrees):
    prow, pcol = point_constants()
    vmem = pl.BlockSpec(memory_space=pltpu.VMEM)
    return pl.pallas_call(
        table_kernel,
        in_specs=[vmem] * 4,
        out_specs=[vmem, vmem, vmem, pl.BlockSpec(memory_space=pltpu.SMEM)],
        out_shape=[
            jax.ShapeDtypeStruct((POINTS + 128, 128), BF16),
            jax.ShapeDtypeStruct((2 * ROWS, 2 * POINTS), BF16),
            jax.ShapeDtypeStruct((3, ROWS, LANES), F32),
            jax.ShapeDtypeStruct((1,), jnp.int32),
        ],
        name="tables",
    )(mode_group[None, :], mode_degrees, jnp.asarray(prow), jnp.asarray(pcol))


def lane_operators():
    source, target = np.meshgrid(np.arange(LANES), np.arange(LANES), indexing="ij")
    gap = source - target
    north = 8.0 * (gap == NZ) - 8.0 * (gap == -NZ) - 1.0 * (gap == 2 * NZ) + 1.0 * (gap == -2 * NZ)
    same_y = source // NZ == target // NZ
    turn = (source - target) % NZ
    laplace = same_y * (1.0 * (turn == 1) + 1.0 * (turn == NZ - 1) - 2.0 * (turn == 0))
    return jnp.asarray(np.stack([np.concatenate([m, m]) for m in (north, laplace)]), BF16)


def pieces_of(value):
    first = value.astype(BF16)
    return first, value - first.astype(F32)


def row_fluxes(fields, eval_ref, proj_ref, lanes_ref):
    points, east, north, source, laplace = [], [], [], [], []
    for value in fields:
        first, second = pieces_of(value)
        both = jnp.concatenate([first, second.astype(BF16)], axis=1)
        laplace.append(jnp.dot(both, lanes_ref[1], preferred_element_type=F32))
        first = first.astype(F32)
        stack = jnp.concatenate([first, second, first, jnp.zeros((8, LANES), F32)], axis=0).astype(BF16)
        result = jnp.dot(eval_ref[...], stack, preferred_element_type=F32)
        points.append(result[0:POINTS])
        east.append(result[POINTS : POINTS + ROWS])
        north.append(result[POINTS + ROWS : POINTS + 2 * ROWS])
        source.append(result[POINTS + 2 * ROWS : POINTS + 3 * ROWS])

    def project(a, b, both):
        product = points[a] * points[b]
        first, second = pieces_of(product)
        stack = jnp.concatenate([first, second.astype(BF16)], axis=0)
        left = proj_ref[...] if both else proj_ref[0:48, :]
        return jnp.dot(left, stack, preferred_element_type=F32)

    def couple(f, result):
        source[f] = source[f] + (3.6 * result[0:ROWS] + (1.08 * math.sqrt(3.0)) * result[ROWS : 2 * ROWS])

    east[0] = east[0] + project(0, 0, False)[0:ROWS]
    result = project(0, 1, True)
    east[1] = east[1] + result[0:ROWS]
    north[0] = north[0] + result[0:ROWS]
    couple(3, result)
    east[2] = east[2] + project(0, 2, False)[0:ROWS]
    result = project(0, 3, True)
    east[3] = east[3] + result[0:ROWS]
    couple(2, result)
    north[1] = north[1] + project(1, 1, False)[0:ROWS]
    result = project(1, 2, True)
    north[2] = north[2] + result[0:ROWS]
    couple(0, result)
    north[3] = north[3] + project(1, 3, False)[0:ROWS]
    couple(1, project(2, 3, True))
    return east, north, source, laplace


def emit_rows(g, rows_of, eval_ref, proj_ref, lanes_ref, scale_ref, east_ref, next_ref, low_ref, high_ref):
    lane = lax.broadcasted_iota(jnp.int32, (1, 128), 1)
    gain = scale_ref[1]
    low, high = [None] * FIELDS, [None] * FIELDS
    for r in range(STEP):
        fields, base, weight = rows_of(r)
        east, north, source, laplace = row_fluxes(fields, eval_ref, proj_ref, lanes_ref)
        here = (lane >= r * STRIP) & (lane < (r + 1) * STRIP)
        for f in range(FIELDS):
            rows = slice(f * ROWS, (f + 1) * ROWS)
            east_ref[STEP * g + r, rows, :] = east[f]
            first, second = pieces_of(north[f])
            slope = jnp.dot(jnp.concatenate([first, second.astype(BF16)], axis=1), lanes_ref[0], preferred_element_type=F32)
            known = gain * (source[f] - slope) + time_step * laplace[f]
            next_ref[STEP * g + r, rows, :] = base[f] + weight * known
            start = pltpu.roll(north[f][:, :128], r * STRIP, 1) if r else north[f][:, :128]
            end = north[f][:, 128:] if r == STEP - 1 else pltpu.roll(north[f][:, 128:], (r + 1) * STRIP, 1)
            low[f] = jnp.where(here, start, low[f]) if r else start
            high[f] = jnp.where(here, end, high[f]) if r else end
    for f in range(FIELDS):
        low_ref[g, f * ROWS : (f + 1) * ROWS, :] = low[f]
        high_ref[g, f * ROWS : (f + 1) * ROWS, :] = high[f]


def from_neighbours(g, r, f, row, low_ref, high_ref):
    rows = slice(f * ROWS, (f + 1) * ROWS)
    total = 8.0 * (row(r + 1, rows) - row(r - 1, rows)) - (row(r + 2, rows) - row(r - 2, rows))
    lane = lax.broadcasted_iota(jnp.int32, (1, 128), 1)
    below, above = high_ref[g, rows, :], low_ref[g, rows, :]
    if r:
        below = pltpu.roll(below, 128 - r * STRIP, 1)
    if r != STEP - 1:
        above = pltpu.roll(above, 96 - r * STRIP, 1)
    low = jnp.where(lane < STRIP, below, 0.0) - jnp.where(lane < NZ, 8.0, 0.0) * pltpu.roll(below, 128 - NZ, 1)
    high = jnp.where(lane >= 128 - NZ, 8.0, 0.0) * pltpu.roll(above, NZ, 1) - jnp.where(lane >= 128 - STRIP, above, 0.0)
    return total + jnp.concatenate([low, high], axis=1)


GROUPS = XROWS // STEP


def over_groups(outer, body):
    lax.fori_loop(0, 2, lambda i, _: (body((GROUPS - 1) * i if outer else 1 + i, i), 0)[1], 0)


def edges_of(east_ref, start_ref, end_ref):
    for k in range(2):
        start_ref[k] = east_ref[k]
        end_ref[k] = east_ref[XROWS - 2 + k]


def first_kernel(outer, *refs):
    state_ref, eval_ref, proj_ref, lanes_ref, scale_ref = refs[:5]
    coef_ref, east_ref, next_ref, low_ref, high_ref = refs[5:10] if outer else refs[10:15]

    def body(g, _):
        def rows_of(r):
            fields = []
            for f in range(FIELDS):
                halves = []
                for half in range(2):
                    full = state_ref[STEP * g + r, pl.ds(FULL_AT + half * SLOTS * FIELDS + f, SLOTS, stride=FIELDS), :]
                    rest = state_ref[STEP * g + r, pl.ds(half * REST * FIELDS + f, SMALL, stride=FIELDS), :]
                    halves.append(jnp.concatenate([full, rest], axis=0))
                value = scale_ref[0] * jnp.concatenate(halves, axis=1)
                coef_ref[STEP * g + r, f * ROWS : (f + 1) * ROWS, :] = value
                fields.append(value)
            return fields, fields, 1.0

        emit_rows(g, rows_of, eval_ref, proj_ref, lanes_ref, scale_ref, east_ref, next_ref, low_ref, high_ref)

    over_groups(outer, body)
    if outer:
        edges_of(east_ref, *refs[10:12])


def side_rows(outer, east_ref, edge_before, edge_after, side_ref):
    if outer:
        side_ref[0, 0:2] = edge_before[...]
        side_ref[0, 2:4] = east_ref[STEP : STEP + 2]
        side_ref[1, 0:2] = east_ref[XROWS - STEP - 2 : XROWS - STEP]
        side_ref[1, 2:4] = edge_after[...]

    def row_at(g, i):
        def row(k, rows):
            if outer and k < 0:
                return side_ref[i, k + 2, rows, :]
            if outer and k >= STEP:
                return side_ref[i, k - STEP + 2, rows, :]
            return east_ref[STEP * g + k, rows, :]

        return row

    return row_at


def middle_kernel(outer, *refs):
    coef_ref, following_ref, from_ref, below_ref, above_ref, eval_ref, proj_ref, lanes_ref, scale_ref = refs[:9]
    if outer:
        edges, (east_ref, next_ref, low_ref, high_ref), ends, side = refs[9:11], refs[15:19], refs[19:21], refs[21]
    else:
        edges, (east_ref, next_ref, low_ref, high_ref), ends, side = (None, None), refs[9:13], None, None
    row_at = side_rows(outer, from_ref, *edges, side)

    def body(g, i):
        def rows_of(r):
            section, base = [], []
            for f in range(FIELDS):
                rows = slice(f * ROWS, (f + 1) * ROWS)
                missing = from_neighbours(g, r, f, row_at(g, i), above_ref, below_ref)
                section.append(following_ref[STEP * g + r, rows, :] - scale_ref[1] * missing)
                base.append(0.5 * (coef_ref[STEP * g + r, rows, :] + section[f]))
            return section, base, 0.5

        emit_rows(g, rows_of, eval_ref, proj_ref, lanes_ref, scale_ref, east_ref, next_ref, low_ref, high_ref)

    over_groups(outer, body)
    if outer:
        edges_of(east_ref, *ends)


def last_kernel(outer, *refs):
    following_ref, from_ref, below_ref, above_ref, scale_ref = refs[:5]
    if outer:
        edges, state_ref, side = refs[5:7], refs[8], refs[9]
    else:
        edges, state_ref, side = (None, None), refs[5], None
    row_at = side_rows(outer, from_ref, *edges, side)

    def body(g, i):
        for r in range(STEP):
            for f in range(FIELDS):
                rows = slice(f * ROWS, (f + 1) * ROWS)
                missing = from_neighbours(g, r, f, row_at(g, i), above_ref, below_ref)
                value = scale_ref[2] * (following_ref[STEP * g + r, rows, :] - 0.5 * scale_ref[1] * missing)
                for half in range(2):
                    lanes = slice(half * 128, (half + 1) * 128)
                    state_ref[STEP * g + r, pl.ds(FULL_AT + half * SLOTS * FIELDS + f, SLOTS, stride=FIELDS), :] = value[:SLOTS, lanes]
                    state_ref[STEP * g + r, pl.ds(half * REST * FIELDS + f, REST, stride=FIELDS), :] = value[SLOTS:MODES, lanes]

    over_groups(outer, body)


TALL = FIELDS * ROWS
ROWS_SHAPE = jax.ShapeDtypeStruct((XROWS, TALL, LANES), F32)
EDGE_SHAPE = jax.ShapeDtypeStruct((2, TALL, LANES), F32)
STRIP_SHAPE = jax.ShapeDtypeStruct((GROUPS, TALL, 128), F32)
PIECES_SHAPE = jax.ShapeDtypeStruct((XROWS, PIECE, 128), F32)


def in_vmem(kernel, ins, outs, name, aliases={}, scratch=()):
    vmem = pl.BlockSpec(memory_space=pltpu.VMEM)
    return pl.pallas_call(
        kernel,
        in_specs=[vmem] * len(ins),
        out_specs=[vmem] * len(outs),
        out_shape=outs,
        input_output_aliases=aliases,
        scratch_shapes=list(scratch),
        compiler_params=pltpu.CompilerParams(vmem_limit_bytes=LIMIT),
        name=name,
    )(*ins)


SIDE = pltpu.VMEM((2, 4, TALL, LANES), F32)


def first_section(tile, tables):
    held = [ROWS_SHAPE] * 3 + [STRIP_SHAPE] * 2
    *outer, start, end = in_vmem(lambda *refs: first_kernel(True, *refs), [tile, *tables], held + [EDGE_SHAPE] * 2, "first_outer")
    known = in_vmem(lambda *refs: first_kernel(False, *refs), [tile, *tables, *outer], held, "first_inner", {5 + i: i for i in range(5)})
    return known, start, end


def second_section(coef, following, east, sides, tables):
    below, above, before, after = sides
    held = [ROWS_SHAPE] * 2 + [STRIP_SHAPE] * 2
    shared = [coef, following, east, below, above, *tables]
    inner = in_vmem(lambda *refs: middle_kernel(False, *refs), shared, held, "second_inner")
    *known, start, end = in_vmem(
        lambda *refs: middle_kernel(True, *refs), [*shared, before, after, *inner], held + [EDGE_SHAPE] * 2, "second_outer", {11 + i: i for i in range(4)}, [SIDE]
    )
    return known, start, end


def advanced(following, east, sides, scale):
    below, above, before, after = sides
    shared = [following, east, below, above, scale]
    (inner,) = in_vmem(lambda *refs: last_kernel(False, *refs), shared, [PIECES_SHAPE], "advanced_inner")
    (tile,) = in_vmem(lambda *refs: last_kernel(True, *refs), [*shared, before, after, inner], [PIECES_SHAPE], "advanced_outer", {7: 0}, [SIDE])
    return tile


CHUNK = 4


def pack_kernel(core_ref, state_ref, out_ref, done):
    copy = pltpu.make_async_copy(state_ref.at[1 - core_ref[0]], out_ref, done)
    copy.start()
    copy.wait()


def merge_kernel(core_ref, big_ref, own_ref, got_ref, out_ref):
    step = pl.program_id(0)
    own_big = core_ref[0] == big_ref[0]

    def put(read, slots, start):
        for block in range(CHUNK):
            for half in range(2):
                for s in range(slots):
                    row = start + (half * slots + s) * FIELDS
                    out_ref[step * CHUNK + block, row : row + FIELDS, :] = read(s, block * LANES + half * 128)

    def own(s, lane):
        return own_ref[0, s, :, lane : lane + 128]

    def got(s, lane):
        return got_ref[s, :, pl.ds(pl.multiple_of(step * (CHUNK * LANES) + lane, 128), 128)]

    @pl.when(own_big)
    def _():
        put(own, SLOTS, FULL_AT)
        put(got, REST, 0)

    @pl.when(jnp.logical_not(own_big))
    def _():
        put(own, REST, 0)
        put(got, SLOTS, FULL_AT)


def split_kernel(core_ref, big_ref, pieces_ref, out_ref, send_ref):
    step = pl.program_id(0)
    own_big = core_ref[0] == big_ref[0]

    def take(slots, start, write):
        for block in range(CHUNK):
            for half in range(2):
                for s in range(SLOTS):
                    row = start + (half * slots + s) * FIELDS
                    value = pieces_ref[step * CHUNK + block, row : row + FIELDS, :] if s < slots else jnp.zeros((FIELDS, 128), F32)
                    write(s, block * LANES + half * 128, value)

    def own(s, lane, value):
        out_ref[0, s, :, lane : lane + 128] = value

    def send(s, lane, value):
        send_ref[s, :, pl.ds(pl.multiple_of(step * (CHUNK * LANES) + lane, 128), 128)] = value

    @pl.when(own_big)
    def _():
        take(SLOTS, FULL_AT, own)
        take(REST, 0, send)

    @pl.when(jnp.logical_not(own_big))
    def _():
        take(REST, 0, own)
        take(SLOTS, FULL_AT, send)


def finish_kernel(core_ref, got_ref, _, out_ref, done):
    copy = pltpu.make_async_copy(got_ref, out_ref.at[1 - core_ref[0]], done)
    copy.start()
    copy.wait()


ROW_SHAPE = jax.ShapeDtypeStruct((SLOTS, FIELDS, 16 * LANES), F32)
STATE_SHAPE = jax.ShapeDtypeStruct((2, SLOTS, FIELDS, 16 * LANES), F32)


def moved(kernel, grid, scalars, ins, outs, shapes, name, aliases={}, scratch=()):
    spec = pltpu.PrefetchScalarGridSpec(num_scalar_prefetch=scalars, grid=grid, in_specs=ins, out_specs=outs, scratch_shapes=list(scratch))
    params = pltpu.CompilerParams(vmem_limit_bytes=LIMIT)
    return pl.pallas_call(kernel, grid_spec=spec, out_shape=shapes, input_output_aliases=aliases, compiler_params=params, name=name)


def movers():
    vmem = pl.BlockSpec(memory_space=pltpu.VMEM)
    anywhere = pl.BlockSpec(memory_space=pl.ANY)
    row = pl.BlockSpec((1, SLOTS, FIELDS, CHUNK * LANES), lambda i, core, *_: (core[0], 0, 0, i))
    grid, semaphore = (16 // CHUNK,), [pltpu.SemaphoreType.DMA]
    pack = moved(pack_kernel, (1,), 1, [anywhere], vmem, ROW_SHAPE, "pack", scratch=semaphore)
    merge = moved(merge_kernel, grid, 2, [row, vmem], vmem, PIECES_SHAPE, "merge")
    split = moved(split_kernel, grid, 2, [vmem], [row, vmem], [STATE_SHAPE, ROW_SHAPE], "split")
    finish = moved(finish_kernel, (1,), 1, [vmem, anywhere], anywhere, STATE_SHAPE, "finish", {2: 0}, semaphore)
    return pack, merge, split, finish


def ring(size, step):
    return [(i, (i + step) % size) for i in range(size)]


def exchange(start, end, low, high):
    size = lax.axis_size("gx_hi")
    before = lax.ppermute(end, "gx_hi", ring(size, 1))
    after = lax.ppermute(start, "gx_hi", ring(size, -1))
    axes = ("gx_lo", "gy", "mode")
    place = [(chip * 2 + side) * 2 + core for side in range(2) for chip in range(8) for core in range(2)]
    up = [(place[i], place[(i + 1) % 32]) for i in range(32)]
    below = lax.ppermute(high, axes, up)
    above = lax.ppermute(low, axes, [(b, a) for a, b in up])
    return below, above, before, after


def shards(chaos_state, mode_group, mode_degrees):
    core = lax.axis_index("mode").astype(jnp.int32).reshape(1)
    pack, merge, split, finish = movers()
    swap = [(0, 1), (1, 0)]
    got = lax.ppermute(pack(core, chaos_state), "mode", swap)
    evaluate, proj, scale, big = make_tables(mode_group, mode_degrees)
    tables = (evaluate, proj, lane_operators(), scale)
    pieces = merge(core, big, chaos_state, got)
    tile = lax.all_to_all(pieces, ("gx_lo", "mode"), 0, 0, tiled=True)
    (coef, east, following, low, high), start, end = first_section(tile, tables)
    sides = exchange(start, end, low, high)
    (east, following, low, high), start, end = second_section(coef, following, east, sides, tables)
    sides = exchange(start, end, low, high)
    tile = advanced(following, east, sides, scale)
    pieces = lax.all_to_all(tile, ("gx_lo", "mode"), 0, 0, tiled=True)
    state, send = split(core, big, pieces)
    return finish(core, lax.ppermute(send, "mode", swap), state)


def solution(mesh):
    fine = Mesh(mesh.devices.reshape(4, 8, 2, 2), ("gx_hi", "gx_lo", "gy", "mode"))
    spec = P(("gx_hi", "gx_lo"), "mode", None, "gy")
    return jax.shard_map(shards, mesh=fine, in_specs=(spec, P(), P()), out_specs=spec, check_vma=False)
```

```python
import math

import jax
import jax.numpy as jnp
import numpy as np
from jax import lax
from jax.experimental import pallas as pl
from jax.experimental.pallas import tpu as pltpu
from jax.sharding import Mesh, PartitionSpec as P

MODES = 35
FIELDS = 4
QUAD = 81
POINTS = 96
NZ = 16
SLOTS = 24
REST = MODES - SLOTS
SMALL = 16
PIECE = 2 * MODES * FIELDS
FULL_AT = 2 * REST * FIELDS
ROWS = SLOTS + SMALL
LANES = 256
STRIP = 2 * NZ
XROWS = 16
STEP = 4
time_step = 0.05
LIMIT = 10 * 1024 * 1024
F32, BF16 = jnp.float32, jnp.bfloat16


def point_constants():
    p = np.arange(POINTS)
    live = (p < QUAD).astype(np.float64)
    digits = [(p // 3**k) % 3 - 1.0 for k in range(4)]
    xi = [math.sqrt(3.0) * d for d in digits]
    weight = live * np.prod([np.where(d == 0, 4.0, 1.0) for d in digits], axis=0)
    east = 1.2 + 0.5 * xi[0]
    north = 0.6 + 0.5 * xi[1]
    decay = -9.6 * np.exp(0.25 * xi[2])
    rows = np.stack(digits + [weight, east, north, decay]).astype(np.float32)
    cols = np.zeros((POINTS, 8), np.float32)
    cols[:, :4] = np.stack(digits, 1)
    cols[:, 4] = live
    return np.concatenate([rows, rows], axis=1), cols


def degree_factor(n, d):
    square = 3.0 * d * d - 1.0
    cubic = d * d * d - d
    return jnp.where(n == 0.0, 1.0, jnp.where(n == 1.0, d, jnp.where(n == 2.0, square, cubic)))


def degree_norm(n):
    third = 3.0 * math.sqrt(3.0) / math.sqrt(6.0)
    return jnp.where(n == 0.0, 1.0, jnp.where(n == 1.0, math.sqrt(3.0), jnp.where(n == 2.0, 1.0 / math.sqrt(2.0), third)))


def table_kernel(group_ref, degrees_ref, prow_ref, pcol_ref, eval_ref, proj_ref, scale_ref, big_ref):
    sub = lax.broadcasted_iota(jnp.int32, (MODES, MODES), 0)
    lane = lax.broadcasted_iota(jnp.int32, (MODES, MODES), 1)
    grow = group_ref[...].astype(F32)
    gcol = jnp.sum(jnp.where(sub == lane, grow, 0.0), axis=1, keepdims=True)
    degrees = degrees_ref[...].astype(F32)
    degrees_t = [jnp.sum(jnp.where(sub == lane, degrees[:, k : k + 1], 0.0), axis=0, keepdims=True) for k in range(4)]
    big_ref[0] = jnp.where(jnp.sum(grow) == float(SLOTS), 1, 0).astype(jnp.int32)
    same = gcol == grow
    rank_row = jnp.sum(jnp.where(same & (sub < lane), 1.0, 0.0), axis=0, keepdims=True)
    rank_col = jnp.sum(jnp.where(same & (lane < sub), 1.0, 0.0), axis=1, keepdims=True)
    ones = jnp.sum(grow, axis=1, keepdims=True)
    big = jnp.where(ones == float(SLOTS), 1.0, 0.0)
    place_row = jnp.where(grow == big, rank_row, rank_row + SLOTS)
    place_col = jnp.where(gcol == big, rank_col, rank_col + SLOTS)
    row_id = lax.broadcasted_iota(jnp.int32, (ROWS, MODES), 0).astype(F32)
    pick = jnp.where(row_id == place_row, 1.0, 0.0)
    live_col = jnp.sum(pick, axis=1, keepdims=True)
    degree_col = [jnp.sum(pick * degrees_t[k], axis=1, keepdims=True) for k in range(4)]
    lane_id = lax.broadcasted_iota(jnp.int32, (MODES, 128), 1)
    lane_row = jnp.where(lane_id < ROWS, lane_id, jnp.where(lane_id < 2 * ROWS, lane_id - ROWS, lane_id - 2 * ROWS)).astype(F32)
    pick_t = jnp.where(lane_row == place_col, 1.0, 0.0)
    live_row = jnp.sum(pick_t, axis=0, keepdims=True)
    degree_row = [jnp.sum(pick_t * degrees[:, k : k + 1], axis=0, keepdims=True) for k in range(4)]
    basis = live_row * pcol_ref[:, 4:5]
    for k in range(4):
        basis = basis * degree_factor(degree_row[k], pcol_ref[:, k : k + 1])
    projector = live_col * prow_ref[4:5, :]
    scale, inverse = live_col, live_col
    for k in range(4):
        projector = projector * degree_factor(degree_col[k], prow_ref[k : k + 1, :])
        norm = degree_norm(degree_col[k])
        scale = scale * norm
        inverse = inverse / norm
    column = lax.broadcasted_iota(jnp.int32, (1, 128), 1)
    eval_ref[0:POINTS, :] = jnp.where(column < 2 * ROWS, basis, 0.0).astype(BF16)
    linear = []
    for k in range(3):
        left = projector[:, :POINTS] * prow_ref[5 + k : 6 + k, :POINTS]
        full = jnp.dot(left, basis, precision=lax.Precision.HIGHEST, preferred_element_type=F32)
        first = full.astype(BF16).astype(F32)
        linear.append(jnp.where(column < 2 * ROWS, first, jnp.where(column < 3 * ROWS, full - first, 0.0)))
    linear.append(jnp.zeros((8, 128), F32))
    eval_ref[POINTS:, :] = jnp.concatenate(linear, axis=0).astype(BF16)
    proj_ref[...] = jnp.concatenate([projector, projector * prow_ref[3:4, :]], axis=0).astype(BF16)
    scale_ref[0] = jnp.broadcast_to(scale, (ROWS, LANES))
    scale_ref[1] = jnp.broadcast_to(scale * scale * (time_step / (24.0 * 1296.0)), (ROWS, LANES))
    scale_ref[2] = jnp.broadcast_to(inverse, (ROWS, LANES))


def make_tables(mode_group, mode_degrees):
    prow, pcol = point_constants()
    vmem = pl.BlockSpec(memory_space=pltpu.VMEM)
    return pl.pallas_call(
        table_kernel,
        in_specs=[vmem] * 4,
        out_specs=[vmem, vmem, vmem, pl.BlockSpec(memory_space=pltpu.SMEM)],
        out_shape=[
            jax.ShapeDtypeStruct((POINTS + 128, 128), BF16),
            jax.ShapeDtypeStruct((2 * ROWS, 2 * POINTS), BF16),
            jax.ShapeDtypeStruct((3, ROWS, LANES), F32),
            jax.ShapeDtypeStruct((1,), jnp.int32),
        ],
        name="tables",
    )(mode_group[None, :], mode_degrees, jnp.asarray(prow), jnp.asarray(pcol))


def lane_operators():
    source, target = np.meshgrid(np.arange(LANES), np.arange(LANES), indexing="ij")
    gap = source - target
    north = 8.0 * (gap == NZ) - 8.0 * (gap == -NZ) - 1.0 * (gap == 2 * NZ) + 1.0 * (gap == -2 * NZ)
    same_y = source // NZ == target // NZ
    turn = (source - target) % NZ
    laplace = same_y * (1.0 * (turn == 1) + 1.0 * (turn == NZ - 1) - 2.0 * (turn == 0))
    return jnp.asarray(np.stack([np.concatenate([m, m]) for m in (north, laplace)]), BF16)


def pieces_of(value):
    first = value.astype(BF16)
    return first, value - first.astype(F32)


def row_fluxes(fields, eval_ref, proj_ref, lanes_ref):
    points, east, north, source, laplace = [], [], [], [], []
    for value in fields:
        first, second = pieces_of(value)
        both = jnp.concatenate([first, second.astype(BF16)], axis=1)
        laplace.append(jnp.dot(both, lanes_ref[1], preferred_element_type=F32))
        first = first.astype(F32)
        stack = jnp.concatenate([first, second, first, jnp.zeros((8, LANES), F32)], axis=0).astype(BF16)
        result = jnp.dot(eval_ref[...], stack, preferred_element_type=F32)
        points.append(result[0:POINTS])
        east.append(result[POINTS : POINTS + ROWS])
        north.append(result[POINTS + ROWS : POINTS + 2 * ROWS])
        source.append(result[POINTS + 2 * ROWS : POINTS + 3 * ROWS])

    def project(a, b, both):
        product = points[a] * points[b]
        first, second = pieces_of(product)
        stack = jnp.concatenate([first, second.astype(BF16)], axis=0)
        left = proj_ref[...] if both else proj_ref[0:48, :]
        return jnp.dot(left, stack, preferred_element_type=F32)

    def couple(f, result):
        source[f] = source[f] + (3.6 * result[0:ROWS] + (1.08 * math.sqrt(3.0)) * result[ROWS : 2 * ROWS])

    east[0] = east[0] + project(0, 0, False)[0:ROWS]
    result = project(0, 1, True)
    east[1] = east[1] + result[0:ROWS]
    north[0] = north[0] + result[0:ROWS]
    couple(3, result)
    east[2] = east[2] + project(0, 2, False)[0:ROWS]
    result = project(0, 3, True)
    east[3] = east[3] + result[0:ROWS]
    couple(2, result)
    north[1] = north[1] + project(1, 1, False)[0:ROWS]
    result = project(1, 2, True)
    north[2] = north[2] + result[0:ROWS]
    couple(0, result)
    north[3] = north[3] + project(1, 3, False)[0:ROWS]
    couple(1, project(2, 3, True))
    return east, north, source, laplace


def emit_rows(core_ref, g, i, rows_of, tables, east_ref, next_ref, inside_ref, outside_ref):
    eval_ref, proj_ref, lanes_ref, scale_ref = tables
    lane = lax.broadcasted_iota(jnp.int32, (1, 128), 1)
    gain = scale_ref[1]
    low, high = [None] * FIELDS, [None] * FIELDS
    for r in range(STEP):
        fields, base, weight = rows_of(r)
        east, north, source, laplace = row_fluxes(fields, eval_ref, proj_ref, lanes_ref)
        here = (lane >= r * STRIP) & (lane < (r + 1) * STRIP)
        for f in range(FIELDS):
            rows = slice(f * ROWS, (f + 1) * ROWS)
            east_ref[STEP * g + r, rows, :] = east[f]
            first, second = pieces_of(north[f])
            slope = jnp.dot(jnp.concatenate([first, second.astype(BF16)], axis=1), lanes_ref[0], preferred_element_type=F32)
            known = gain * (source[f] - slope) + time_step * laplace[f]
            next_ref[STEP * g + r, rows, :] = base[f] + weight * known
            start = pltpu.roll(north[f][:, :128], r * STRIP, 1) if r else north[f][:, :128]
            end = north[f][:, 128:] if r == STEP - 1 else pltpu.roll(north[f][:, 128:], (r + 1) * STRIP, 1)
            low[f] = jnp.where(here, start, low[f]) if r else start
            high[f] = jnp.where(here, end, high[f]) if r else end

    def store(inside, outside):
        for f in range(FIELDS):
            inside_ref[i, f * ROWS : (f + 1) * ROWS, :] = inside[f]
            outside_ref[i, f * ROWS : (f + 1) * ROWS, :] = outside[f]

    pl.when(core_ref[0] == 0)(lambda: store(high, low))
    pl.when(core_ref[0] == 1)(lambda: store(low, high))


def from_neighbours(i, r, f, row, strips):
    rows = slice(f * ROWS, (f + 1) * ROWS)
    total = 8.0 * (row(r + 1, rows) - row(r - 1, rows)) - (row(r + 2, rows) - row(r - 2, rows))
    lane = lax.broadcasted_iota(jnp.int32, (1, 128), 1)
    below, above = strips[0, i, rows, :], strips[1, i, rows, :]
    if r:
        below = pltpu.roll(below, 128 - r * STRIP, 1)
    if r != STEP - 1:
        above = pltpu.roll(above, 96 - r * STRIP, 1)
    low = jnp.where(lane < STRIP, below, 0.0) - jnp.where(lane < NZ, 8.0, 0.0) * pltpu.roll(below, 128 - NZ, 1)
    high = jnp.where(lane >= 128 - NZ, 8.0, 0.0) * pltpu.roll(above, NZ, 1) - jnp.where(lane >= 128 - STRIP, above, 0.0)
    return total + jnp.concatenate([low, high], axis=1)


GROUPS = XROWS // STEP


def over_groups(outer, body):
    lax.fori_loop(0, 2, lambda i, _: (body((GROUPS - 1) * i if outer else 1 + i, i), 0)[1], 0)


def edges_of(east_ref, start_ref, end_ref):
    for k in range(2):
        start_ref[k] = east_ref[k]
        end_ref[k] = east_ref[XROWS - 2 + k]


def first_kernel(outer, core_ref, *refs):
    state_ref, tables = refs[0], refs[1:5]
    coef_ref, east_ref, next_ref, inside_ref, outside_ref = refs[5:10] if outer else refs[8:13]

    def body(g, i):
        def rows_of(r):
            fields = []
            for f in range(FIELDS):
                halves = []
                for half in range(2):
                    full = state_ref[STEP * g + r, pl.ds(FULL_AT + half * SLOTS * FIELDS + f, SLOTS, stride=FIELDS), :]
                    rest = state_ref[STEP * g + r, pl.ds(half * REST * FIELDS + f, SMALL, stride=FIELDS), :]
                    halves.append(jnp.concatenate([full, rest], axis=0))
                value = tables[3][0] * jnp.concatenate(halves, axis=1)
                coef_ref[STEP * g + r, f * ROWS : (f + 1) * ROWS, :] = value
                fields.append(value)
            return fields, fields, 1.0

        emit_rows(core_ref, g, i, rows_of, tables, east_ref, next_ref, inside_ref, outside_ref)

    over_groups(outer, body)
    if outer:
        edges_of(east_ref, *refs[10:12])


def neighbour_strips(core_ref, inside_ref, outside_ref, strips):
    def hold(below_ref, above_ref):
        strips[0] = below_ref[...]
        strips[1] = above_ref[...]

    pl.when(core_ref[0] == 0)(lambda: hold(outside_ref, inside_ref))
    pl.when(core_ref[0] == 1)(lambda: hold(inside_ref, outside_ref))


def side_rows(outer, east_ref, edge_before, edge_after, side_ref):
    if outer:
        side_ref[0, 0:2] = edge_before[...]
        side_ref[0, 2:4] = east_ref[STEP : STEP + 2]
        side_ref[1, 0:2] = east_ref[XROWS - STEP - 2 : XROWS - STEP]
        side_ref[1, 2:4] = edge_after[...]

    def row_at(g, i):
        def row(k, rows):
            if outer and k < 0:
                return side_ref[i, k + 2, rows, :]
            if outer and k >= STEP:
                return side_ref[i, k - STEP + 2, rows, :]
            return east_ref[STEP * g + k, rows, :]

        return row

    return row_at


def middle_kernel(outer, core_ref, *refs):
    coef_ref, following_ref, from_ref, inside_from, outside_from = refs[:5]
    tables = refs[5:9]
    if outer:
        edges, (east_ref, next_ref, inside_ref, outside_ref), ends, (strips, side) = refs[9:11], refs[11:15], refs[15:17], refs[17:]
    else:
        edges, (east_ref, next_ref, inside_ref, outside_ref), ends, (strips, side) = (None, None), refs[11:15], None, (refs[15], None)
    row_at = side_rows(outer, from_ref, *edges, side)
    neighbour_strips(core_ref, inside_from, outside_from, strips)

    def body(g, i):
        def rows_of(r):
            section, base = [], []
            for f in range(FIELDS):
                rows = slice(f * ROWS, (f + 1) * ROWS)
                missing = from_neighbours(i, r, f, row_at(g, i), strips)
                section.append(following_ref[STEP * g + r, rows, :] - tables[3][1] * missing)
                base.append(0.5 * (coef_ref[STEP * g + r, rows, :] + section[f]))
            return section, base, 0.5

        emit_rows(core_ref, g, i, rows_of, tables, east_ref, next_ref, inside_ref, outside_ref)

    over_groups(outer, body)
    if outer:
        edges_of(east_ref, *ends)


def last_kernel(outer, core_ref, *refs):
    following_ref, from_ref, inside_from, outside_from, scale_ref = refs[:5]
    if outer:
        edges, state_ref, (strips, side) = refs[5:7], refs[7], refs[8:]
    else:
        edges, state_ref, (strips, side) = (None, None), refs[6], (refs[7], None)
    row_at = side_rows(outer, from_ref, *edges, side)
    neighbour_strips(core_ref, inside_from, outside_from, strips)

    def body(g, i):
        for r in range(STEP):
            for f in range(FIELDS):
                rows = slice(f * ROWS, (f + 1) * ROWS)
                missing = from_neighbours(i, r, f, row_at(g, i), strips)
                value = scale_ref[2] * (following_ref[STEP * g + r, rows, :] - 0.5 * scale_ref[1] * missing)
                for half in range(2):
                    lanes = slice(half * 128, (half + 1) * 128)
                    state_ref[STEP * g + r, pl.ds(FULL_AT + half * SLOTS * FIELDS + f, SLOTS, stride=FIELDS), :] = value[:SLOTS, lanes]
                    state_ref[STEP * g + r, pl.ds(half * REST * FIELDS + f, REST, stride=FIELDS), :] = value[SLOTS:MODES, lanes]

    over_groups(outer, body)


TALL = FIELDS * ROWS
ROWS_SHAPE = jax.ShapeDtypeStruct((XROWS, TALL, LANES), F32)
EDGE_SHAPE = jax.ShapeDtypeStruct((2, TALL, LANES), F32)
STRIP_SHAPE = jax.ShapeDtypeStruct((2, TALL, 128), F32)
PIECES_SHAPE = jax.ShapeDtypeStruct((XROWS, PIECE, 128), F32)
SIDE = pltpu.VMEM((2, 4, TALL, LANES), F32)
STRIPS = pltpu.VMEM((2, 2, TALL, 128), F32)


def in_vmem(kernel, core, ins, outs, name, cost, aliases={}, scratch=()):
    vmem = pl.BlockSpec(memory_space=pltpu.VMEM)
    return pl.pallas_call(
        kernel,
        in_specs=[pl.BlockSpec(memory_space=pltpu.SMEM)] + [vmem] * len(ins),
        out_specs=[vmem] * len(outs),
        out_shape=outs,
        input_output_aliases={1 + i: o for i, o in aliases.items()},
        scratch_shapes=list(scratch),
        cost_estimate=pl.CostEstimate(flops=int(cost * 1e9), bytes_accessed=int(cost * 3e6), transcendentals=0),
        compiler_params=pltpu.CompilerParams(vmem_limit_bytes=LIMIT),
        name=name,
    )(core, *ins)


def first_section(core, tile, tables):
    def run(outer):
        return lambda *refs: first_kernel(outer, *refs)

    held, strips = [ROWS_SHAPE] * 3, [STRIP_SHAPE] * 2
    *known, inside, outside, start, end = in_vmem(run(True), core, [tile, *tables], held + strips + [EDGE_SHAPE] * 2, "first_outer", 5)
    outer = exchange_x(start, end) + exchange_y(inside, outside)
    *known, inside, outside = in_vmem(run(False), core, [tile, *tables, *known], held + strips, "first_inner", 20, {5: 0, 6: 1, 7: 2})
    return known, outer, exchange_y(inside, outside)


def second_section(core, coef, following, east, outer, inner, tables):
    def run(outer):
        return lambda *refs: middle_kernel(outer, *refs)

    held, strips = [ROWS_SHAPE] * 2, [STRIP_SHAPE] * 2
    shared = [coef, following, east]
    ins = [*shared, *outer[2:], *tables, *outer[:2]]
    *known, inside, outside, start, end = in_vmem(run(True), core, ins, held + strips + [EDGE_SHAPE] * 2, "second_outer", 8, scratch=[STRIPS, SIDE])
    outer = exchange_x(start, end) + exchange_y(inside, outside)
    ins = [*shared, *inner, *tables, *known]
    *known, inside, outside = in_vmem(run(False), core, ins, held + strips, "second_inner", 20, {9: 0, 10: 1}, [STRIPS])
    return known, outer, exchange_y(inside, outside)


def advanced(core, following, east, outer, inner, scale):
    def run(outer):
        return lambda *refs: last_kernel(outer, *refs)

    ins = [following, east, *outer[2:], scale, *outer[:2]]
    (tile,) = in_vmem(run(True), core, ins, [PIECES_SHAPE], "advanced_outer", 8, scratch=[STRIPS, SIDE])
    ins = [following, east, *inner, scale, tile]
    (tile,) = in_vmem(run(False), core, ins, [PIECES_SHAPE], "advanced_inner", 8, {5: 0}, [STRIPS])
    return tile


CHUNK = 4


def pack_kernel(core_ref, state_ref, out_ref, done):
    copy = pltpu.make_async_copy(state_ref.at[1 - core_ref[0]], out_ref, done)
    copy.start()
    copy.wait()


def merge_kernel(core_ref, big_ref, own_ref, got_ref, out_ref):
    step = pl.program_id(0)
    own_big = core_ref[0] == big_ref[0]

    def put(read, slots, start):
        for block in range(CHUNK):
            for half in range(2):
                for s in range(slots):
                    row = start + (half * slots + s) * FIELDS
                    out_ref[step * CHUNK + block, row : row + FIELDS, :] = read(s, block * LANES + half * 128)

    def own(s, lane):
        return own_ref[0, s, :, lane : lane + 128]

    def got(s, lane):
        return got_ref[s, :, pl.ds(pl.multiple_of(step * (CHUNK * LANES) + lane, 128), 128)]

    @pl.when(own_big)
    def _():
        put(own, SLOTS, FULL_AT)
        put(got, REST, 0)

    @pl.when(jnp.logical_not(own_big))
    def _():
        put(own, REST, 0)
        put(got, SLOTS, FULL_AT)


def split_kernel(core_ref, big_ref, pieces_ref, out_ref, send_ref):
    step = pl.program_id(0)
    own_big = core_ref[0] == big_ref[0]

    def take(slots, start, write):
        for block in range(CHUNK):
            for half in range(2):
                for s in range(SLOTS):
                    row = start + (half * slots + s) * FIELDS
                    value = pieces_ref[step * CHUNK + block, row : row + FIELDS, :] if s < slots else jnp.zeros((FIELDS, 128), F32)
                    write(s, block * LANES + half * 128, value)

    def own(s, lane, value):
        out_ref[0, s, :, lane : lane + 128] = value

    def send(s, lane, value):
        send_ref[s, :, pl.ds(pl.multiple_of(step * (CHUNK * LANES) + lane, 128), 128)] = value

    @pl.when(own_big)
    def _():
        take(SLOTS, FULL_AT, own)
        take(REST, 0, send)

    @pl.when(jnp.logical_not(own_big))
    def _():
        take(REST, 0, own)
        take(SLOTS, FULL_AT, send)


def finish_kernel(core_ref, got_ref, _, out_ref, done):
    copy = pltpu.make_async_copy(got_ref, out_ref.at[1 - core_ref[0]], done)
    copy.start()
    copy.wait()


ROW_SHAPE = jax.ShapeDtypeStruct((SLOTS, FIELDS, 16 * LANES), F32)
STATE_SHAPE = jax.ShapeDtypeStruct((2, SLOTS, FIELDS, 16 * LANES), F32)


def moved(kernel, grid, scalars, ins, outs, shapes, name, aliases={}, scratch=()):
    spec = pltpu.PrefetchScalarGridSpec(num_scalar_prefetch=scalars, grid=grid, in_specs=ins, out_specs=outs, scratch_shapes=list(scratch))
    params = pltpu.CompilerParams(vmem_limit_bytes=LIMIT)
    return pl.pallas_call(kernel, grid_spec=spec, out_shape=shapes, input_output_aliases=aliases, compiler_params=params, name=name)


def movers():
    vmem = pl.BlockSpec(memory_space=pltpu.VMEM)
    anywhere = pl.BlockSpec(memory_space=pltpu.HBM)
    row = pl.BlockSpec((1, SLOTS, FIELDS, CHUNK * LANES), lambda i, core, *_: (core[0], 0, 0, i))
    grid, semaphore = (16 // CHUNK,), [pltpu.SemaphoreType.DMA]
    pack = moved(pack_kernel, (1,), 1, [anywhere], vmem, ROW_SHAPE, "pack", scratch=semaphore)
    merge = moved(merge_kernel, grid, 2, [row, vmem], vmem, PIECES_SHAPE, "merge")
    split = moved(split_kernel, grid, 2, [vmem], [row, vmem], [STATE_SHAPE, ROW_SHAPE], "split")
    finish = moved(finish_kernel, (1,), 1, [vmem, anywhere], anywhere, STATE_SHAPE, "finish", {2: 0}, semaphore)
    return pack, merge, split, finish


def ring(size, step):
    return [(i, (i + step) % size) for i in range(size)]


def exchange_x(start, end):
    size = lax.axis_size("gx_hi")
    return lax.ppermute(end, "gx_hi", ring(size, 1)), lax.ppermute(start, "gx_hi", ring(size, -1))


def exchange_y(inside, outside):
    place = [(chip * 2 + side) * 2 + core for side in range(2) for chip in range(8) for core in range(2)]
    pairs = [(place[i], place[(i + 1) % 32]) for i in range(1, 32, 2)]
    swap = pairs + [(b, a) for a, b in pairs]
    return lax.ppermute(inside, "mode", [(0, 1), (1, 0)]), lax.ppermute(outside, ("gx_lo", "gy", "mode"), swap)


def shards(chaos_state, mode_group, mode_degrees):
    core = lax.axis_index("mode").astype(jnp.int32).reshape(1)
    pack, merge, split, finish = movers()
    swap = [(0, 1), (1, 0)]
    got = lax.ppermute(pack(core, chaos_state), "mode", swap)
    evaluate, proj, scale, big = make_tables(mode_group, mode_degrees)
    tables = (evaluate, proj, lane_operators(), scale)
    pieces = merge(core, big, chaos_state, got)
    tile = lax.all_to_all(pieces, ("gx_lo", "mode"), 0, 0, tiled=True)
    (coef, east, following), outer, inner = first_section(core, tile, tables)
    (east, following), outer, inner = second_section(core, coef, following, east, outer, inner, tables)
    tile = advanced(core, following, east, outer, inner, scale)
    pieces = lax.all_to_all(tile, ("gx_lo", "mode"), 0, 0, tiled=True)
    state, send = split(core, big, pieces)
    return finish(core, lax.ppermute(send, "mode", swap), state)


def solution(mesh):
    fine = Mesh(mesh.devices.reshape(4, 8, 2, 2), ("gx_hi", "gx_lo", "gy", "mode"))
    spec = P(("gx_hi", "gx_lo"), "mode", None, "gy")
    return jax.shard_map(shards, mesh=fine, in_specs=(spec, P(), P()), out_specs=spec, check_vma=False)
```

```python
import math

import jax
import jax.numpy as jnp
import numpy as np
from jax import lax
from jax.experimental import pallas as pl
from jax.experimental.pallas import tpu as pltpu
from jax.sharding import Mesh, PartitionSpec as P

MODES = 35
FIELDS = 4
QUAD = 81
POINTS = 96
NZ = 16
SLOTS = 24
REST = MODES - SLOTS
SMALL = 16
BLOCKS = 16
HALVES = 2 * FIELDS
PIECE = MODES * HALVES
FULL_AT = REST * HALVES
ROWS = SLOTS + SMALL
LANES = 256
STRIP = 2 * NZ
XROWS = 16
STEP = 4
time_step = 0.05
LIMIT = 10 * 1024 * 1024
F32, BF16 = jnp.float32, jnp.bfloat16


def point_constants():
    p = np.arange(POINTS)
    live = (p < QUAD).astype(np.float64)
    digits = [(p // 3**k) % 3 - 1.0 for k in range(4)]
    xi = [math.sqrt(3.0) * d for d in digits]
    weight = live * np.prod([np.where(d == 0, 4.0, 1.0) for d in digits], axis=0)
    east = 1.2 + 0.5 * xi[0]
    north = 0.6 + 0.5 * xi[1]
    decay = -9.6 * np.exp(0.25 * xi[2])
    rows = np.stack(digits + [weight, east, north, decay]).astype(np.float32)
    cols = np.zeros((POINTS, 8), np.float32)
    cols[:, :4] = np.stack(digits, 1)
    cols[:, 4] = live
    return np.concatenate([rows, rows], axis=1), cols


def degree_factor(n, d):
    square = 3.0 * d * d - 1.0
    cubic = d * d * d - d
    return jnp.where(n == 0.0, 1.0, jnp.where(n == 1.0, d, jnp.where(n == 2.0, square, cubic)))


def degree_norm(n):
    third = 3.0 * math.sqrt(3.0) / math.sqrt(6.0)
    return jnp.where(n == 0.0, 1.0, jnp.where(n == 1.0, math.sqrt(3.0), jnp.where(n == 2.0, 1.0 / math.sqrt(2.0), third)))


def table_kernel(group_ref, degrees_ref, prow_ref, pcol_ref, eval_ref, proj_ref, scale_ref, big_ref):
    sub = lax.broadcasted_iota(jnp.int32, (MODES, MODES), 0)
    lane = lax.broadcasted_iota(jnp.int32, (MODES, MODES), 1)
    grow = group_ref[...].astype(F32)
    gcol = jnp.sum(jnp.where(sub == lane, grow, 0.0), axis=1, keepdims=True)
    degrees = degrees_ref[...].astype(F32)
    degrees_t = [jnp.sum(jnp.where(sub == lane, degrees[:, k : k + 1], 0.0), axis=0, keepdims=True) for k in range(4)]
    big_ref[0] = jnp.where(jnp.sum(grow) == float(SLOTS), 1, 0).astype(jnp.int32)
    same = gcol == grow
    rank_row = jnp.sum(jnp.where(same & (sub < lane), 1.0, 0.0), axis=0, keepdims=True)
    rank_col = jnp.sum(jnp.where(same & (lane < sub), 1.0, 0.0), axis=1, keepdims=True)
    ones = jnp.sum(grow, axis=1, keepdims=True)
    big = jnp.where(ones == float(SLOTS), 1.0, 0.0)
    place_row = jnp.where(grow == big, rank_row, rank_row + SLOTS)
    place_col = jnp.where(gcol == big, rank_col, rank_col + SLOTS)
    row_id = lax.broadcasted_iota(jnp.int32, (ROWS, MODES), 0).astype(F32)
    pick = jnp.where(row_id == place_row, 1.0, 0.0)
    live_col = jnp.sum(pick, axis=1, keepdims=True)
    degree_col = [jnp.sum(pick * degrees_t[k], axis=1, keepdims=True) for k in range(4)]
    lane_id = lax.broadcasted_iota(jnp.int32, (MODES, 128), 1)
    lane_row = jnp.where(lane_id < ROWS, lane_id, jnp.where(lane_id < 2 * ROWS, lane_id - ROWS, lane_id - 2 * ROWS)).astype(F32)
    pick_t = jnp.where(lane_row == place_col, 1.0, 0.0)
    live_row = jnp.sum(pick_t, axis=0, keepdims=True)
    degree_row = [jnp.sum(pick_t * degrees[:, k : k + 1], axis=0, keepdims=True) for k in range(4)]
    basis = live_row * pcol_ref[:, 4:5]
    for k in range(4):
        basis = basis * degree_factor(degree_row[k], pcol_ref[:, k : k + 1])
    projector = live_col * prow_ref[4:5, :]
    scale, inverse = live_col, live_col
    for k in range(4):
        projector = projector * degree_factor(degree_col[k], prow_ref[k : k + 1, :])
        norm = degree_norm(degree_col[k])
        scale = scale * norm
        inverse = inverse / norm
    column = lax.broadcasted_iota(jnp.int32, (1, 128), 1)
    eval_ref[0:POINTS, :] = jnp.where(column < 2 * ROWS, basis, 0.0).astype(BF16)
    linear = []
    for k in range(3):
        left = projector[:, :POINTS] * prow_ref[5 + k : 6 + k, :POINTS]
        full = jnp.dot(left, basis, precision=lax.Precision.HIGHEST, preferred_element_type=F32)
        first = full.astype(BF16).astype(F32)
        linear.append(jnp.where(column < 2 * ROWS, first, jnp.where(column < 3 * ROWS, full - first, 0.0)))
    linear.append(jnp.zeros((8, 128), F32))
    eval_ref[POINTS:, :] = jnp.concatenate(linear, axis=0).astype(BF16)
    proj_ref[...] = jnp.concatenate([projector, projector * prow_ref[3:4, :]], axis=0).astype(BF16)
    scale_ref[0] = jnp.broadcast_to(scale, (ROWS, LANES))
    scale_ref[1] = jnp.broadcast_to(scale * scale * (time_step / (24.0 * 1296.0)), (ROWS, LANES))
    scale_ref[2] = jnp.broadcast_to(inverse, (ROWS, LANES))


def make_tables(mode_group, mode_degrees):
    prow, pcol = point_constants()
    vmem = pl.BlockSpec(memory_space=pltpu.VMEM)
    return pl.pallas_call(
        table_kernel,
        in_specs=[vmem] * 4,
        out_specs=[vmem, vmem, vmem, pl.BlockSpec(memory_space=pltpu.SMEM)],
        out_shape=[
            jax.ShapeDtypeStruct((POINTS + 128, 128), BF16),
            jax.ShapeDtypeStruct((2 * ROWS, 2 * POINTS), BF16),
            jax.ShapeDtypeStruct((3, ROWS, LANES), F32),
            jax.ShapeDtypeStruct((1,), jnp.int32),
        ],
        name="tables",
    )(mode_group[None, :], mode_degrees, jnp.asarray(prow), jnp.asarray(pcol))


def lane_operators():
    source, target = np.meshgrid(np.arange(LANES), np.arange(LANES), indexing="ij")
    gap = source - target
    north = 8.0 * (gap == NZ) - 8.0 * (gap == -NZ) - 1.0 * (gap == 2 * NZ) + 1.0 * (gap == -2 * NZ)
    same_y = source // NZ == target // NZ
    turn = (source - target) % NZ
    laplace = same_y * (1.0 * (turn == 1) + 1.0 * (turn == NZ - 1) - 2.0 * (turn == 0))
    return jnp.asarray(np.stack([np.concatenate([m, m]) for m in (north, laplace)]), BF16)


def pieces_of(value):
    first = value.astype(BF16)
    return first, value - first.astype(F32)


def by_lanes(value, operator):
    first, second = pieces_of(value)
    return first, second, jnp.dot(jnp.concatenate([first, second.astype(BF16)], axis=1), operator, preferred_element_type=F32)


def row_fluxes(fields, eval_ref, proj_ref, lanes_ref):
    points, east, north, source = [], [], [], []
    first, second, laplace = by_lanes(jnp.concatenate(fields, axis=0), lanes_ref[1])
    first = first.astype(F32)
    for f in range(FIELDS):
        rows = slice(f * ROWS, (f + 1) * ROWS)
        stack = jnp.concatenate([first[rows], second[rows], first[rows], jnp.zeros((8, LANES), F32)], axis=0).astype(BF16)
        result = jnp.dot(eval_ref[...], stack, preferred_element_type=F32)
        points.append(result[0:POINTS])
        east.append(result[POINTS : POINTS + ROWS])
        north.append(result[POINTS + ROWS : POINTS + 2 * ROWS])
        source.append(result[POINTS + 2 * ROWS : POINTS + 3 * ROWS])

    def project(a, b, both):
        product = points[a] * points[b]
        first, second = pieces_of(product)
        stack = jnp.concatenate([first, second.astype(BF16)], axis=0)
        left = proj_ref[...] if both else proj_ref[0:48, :]
        return jnp.dot(left, stack, preferred_element_type=F32)

    def couple(f, result):
        source[f] = source[f] + (3.6 * result[0:ROWS] + (1.08 * math.sqrt(3.0)) * result[ROWS : 2 * ROWS])

    east[0] = east[0] + project(0, 0, False)[0:ROWS]
    result = project(0, 1, True)
    east[1] = east[1] + result[0:ROWS]
    north[0] = north[0] + result[0:ROWS]
    couple(3, result)
    east[2] = east[2] + project(0, 2, False)[0:ROWS]
    result = project(0, 3, True)
    east[3] = east[3] + result[0:ROWS]
    couple(2, result)
    north[1] = north[1] + project(1, 1, False)[0:ROWS]
    result = project(1, 2, True)
    north[2] = north[2] + result[0:ROWS]
    couple(0, result)
    north[3] = north[3] + project(1, 3, False)[0:ROWS]
    couple(1, project(2, 3, True))
    return east, north, source, laplace


def emit_rows(core_ref, g, at, rows_of, tables, east_ref, next_ref, inside_ref, outside_ref):
    eval_ref, proj_ref, lanes_ref, scale_ref = tables
    lane = lax.broadcasted_iota(jnp.int32, (1, 128), 1)
    gain = scale_ref[1]
    low, high = [None] * FIELDS, [None] * FIELDS
    for r in range(STEP):
        fields, base, weight = rows_of(r)
        east, north, source, laplace = row_fluxes(fields, eval_ref, proj_ref, lanes_ref)
        here = (lane >= r * STRIP) & (lane < (r + 1) * STRIP)
        slope = by_lanes(jnp.concatenate(north, axis=0), lanes_ref[0])[2]
        for f in range(FIELDS):
            rows = slice(f * ROWS, (f + 1) * ROWS)
            east_ref[STEP * g + r, rows, :] = east[f]
            known = gain * (source[f] - slope[rows]) + time_step * laplace[rows]
            next_ref[STEP * g + r, rows, :] = base[f] + weight * known
            start = pltpu.roll(north[f][:, :128], r * STRIP, 1) if r else north[f][:, :128]
            end = north[f][:, 128:] if r == STEP - 1 else pltpu.roll(north[f][:, 128:], (r + 1) * STRIP, 1)
            low[f] = jnp.where(here, start, low[f]) if r else start
            high[f] = jnp.where(here, end, high[f]) if r else end

    def store(inside, outside):
        for f in range(FIELDS):
            inside_ref[at, f * ROWS : (f + 1) * ROWS, :] = inside[f]
            outside_ref[at, f * ROWS : (f + 1) * ROWS, :] = outside[f]

    pl.when(core_ref[0] == 0)(lambda: store(high, low))
    pl.when(core_ref[0] == 1)(lambda: store(low, high))


def from_neighbours(i, r, f, row, strips):
    rows = slice(f * ROWS, (f + 1) * ROWS)
    total = 8.0 * (row(r + 1, rows) - row(r - 1, rows)) - (row(r + 2, rows) - row(r - 2, rows))
    lane = lax.broadcasted_iota(jnp.int32, (1, 128), 1)
    below, above = strips[0, i, rows, :], strips[1, i, rows, :]
    if r:
        below = pltpu.roll(below, 128 - r * STRIP, 1)
    if r != STEP - 1:
        above = pltpu.roll(above, 96 - r * STRIP, 1)
    low = jnp.where(lane < STRIP, below, 0.0) - jnp.where(lane < NZ, 8.0, 0.0) * pltpu.roll(below, 128 - NZ, 1)
    high = jnp.where(lane >= 128 - NZ, 8.0, 0.0) * pltpu.roll(above, NZ, 1) - jnp.where(lane >= 128 - STRIP, above, 0.0)
    return total + jnp.concatenate([low, high], axis=1)


GROUPS = XROWS // STEP


def over_groups(outer, body):
    lax.fori_loop(0, 2, lambda i, _: (body((GROUPS - 1) * i if outer else 1 + i, i), 0)[1], 0)


def edges_of(east_ref, start_ref, end_ref):
    for k in range(2):
        start_ref[k] = east_ref[k]
        end_ref[k] = east_ref[XROWS - 2 + k]


def first_kernel(outer, core_ref, *refs):
    state_ref, tables = refs[0], refs[1:5]
    coef_ref, east_ref, next_ref, inside_ref, outside_ref = refs[5:10] if outer else refs[8:13]

    def body(g, i):
        def rows_of(r):
            fields = []
            for f in range(FIELDS):
                halves = []
                for half in range(2):
                    full = state_ref[STEP * g + r, pl.ds(FULL_AT + half * FIELDS + f, SLOTS, stride=HALVES), :]
                    rest = state_ref[STEP * g + r, pl.ds(half * FIELDS + f, SMALL, stride=HALVES), :]
                    halves.append(jnp.concatenate([full, rest], axis=0))
                value = tables[3][0] * jnp.concatenate(halves, axis=1)
                coef_ref[STEP * g + r, f * ROWS : (f + 1) * ROWS, :] = value
                fields.append(value)
            return fields, fields, 1.0

        emit_rows(core_ref, g, i, rows_of, tables, east_ref, next_ref, inside_ref, outside_ref)

    over_groups(outer, body)
    if outer:
        edges_of(east_ref, *refs[10:12])


def neighbour_strips(core_ref, inside_ref, outside_ref, strips):
    def hold(below_ref, above_ref):
        strips[0] = below_ref[...]
        strips[1] = above_ref[...]

    pl.when(core_ref[0] == 0)(lambda: hold(outside_ref, inside_ref))
    pl.when(core_ref[0] == 1)(lambda: hold(inside_ref, outside_ref))


def side_rows(outer, east_ref, edge_before, edge_after, side_ref):
    if outer:
        side_ref[0, 0:2] = edge_before[...]
        side_ref[0, 2:4] = east_ref[STEP : STEP + 2]
        side_ref[1, 0:2] = east_ref[XROWS - STEP - 2 : XROWS - STEP]
        side_ref[1, 2:4] = edge_after[...]

    def row_at(g, i):
        def row(k, rows):
            if outer and k < 0:
                return side_ref[i, k + 2, rows, :]
            if outer and k >= STEP:
                return side_ref[i, k - STEP + 2, rows, :]
            return east_ref[STEP * g + k, rows, :]

        return row

    return row_at


def middle_kernel(outer, core_ref, *refs):
    coef_ref, following_ref, from_ref, inside_from, outside_from = refs[:5]
    tables = refs[5:9]
    if outer:
        edges, (east_ref, next_ref, inside_ref, outside_ref), ends, (strips, side) = refs[9:11], refs[11:15], refs[15:17], refs[17:]
    else:
        edges, (east_ref, next_ref, inside_ref, outside_ref), ends, (strips, side) = (None, None), refs[13:17], None, (refs[17], None)
        for given, held in ((refs[11], inside_ref), (refs[12], outside_ref)):
            held[0] = given[0]
            held[GROUPS - 1] = given[1]
    row_at = side_rows(outer, from_ref, *edges, side)
    neighbour_strips(core_ref, inside_from, outside_from, strips)

    def body(g, i):
        def rows_of(r):
            section, base = [], []
            for f in range(FIELDS):
                rows = slice(f * ROWS, (f + 1) * ROWS)
                missing = from_neighbours(i, r, f, row_at(g, i), strips)
                section.append(following_ref[STEP * g + r, rows, :] - tables[3][1] * missing)
                base.append(0.5 * (coef_ref[STEP * g + r, rows, :] + section[f]))
            return section, base, 0.5

        emit_rows(core_ref, g, i if outer else g, rows_of, tables, east_ref, next_ref, inside_ref, outside_ref)

    over_groups(outer, body)
    if outer:
        edges_of(east_ref, *ends)


def last_kernel(core_ref, following_ref, from_ref, inside_from, outside_from, scale_ref, edge_before, edge_after, state_ref, strips, side):
    neighbour_strips(core_ref, inside_from, outside_from, strips)
    for outer in (True, False):
        row_at = side_rows(outer, from_ref, edge_before, edge_after, side)

        def body(g, i):
            for r in range(STEP):
                for f in range(FIELDS):
                    rows = slice(f * ROWS, (f + 1) * ROWS)
                    missing = from_neighbours(g, r, f, row_at(g, i), strips)
                    value = scale_ref[2] * (following_ref[STEP * g + r, rows, :] - 0.5 * scale_ref[1] * missing)
                    for half in range(2):
                        lanes = slice(half * 128, (half + 1) * 128)
                        state_ref[STEP * g + r, pl.ds(FULL_AT + half * FIELDS + f, SLOTS, stride=HALVES), :] = value[:SLOTS, lanes]
                        state_ref[STEP * g + r, pl.ds(half * FIELDS + f, REST, stride=HALVES), :] = value[SLOTS:MODES, lanes]

        over_groups(outer, body)


TALL = FIELDS * ROWS
ROWS_SHAPE = jax.ShapeDtypeStruct((XROWS, TALL, LANES), F32)
EDGE_SHAPE = jax.ShapeDtypeStruct((2, TALL, LANES), F32)
STRIP_SHAPE = jax.ShapeDtypeStruct((2, TALL, 128), F32)
STRIPS_SHAPE = jax.ShapeDtypeStruct((GROUPS, TALL, 128), F32)
PIECES_SHAPE = jax.ShapeDtypeStruct((XROWS, PIECE, 128), F32)
SIDE = pltpu.VMEM((2, 4, TALL, LANES), F32)
STRIPS = pltpu.VMEM((2, 2, TALL, 128), F32)
ALL_STRIPS = pltpu.VMEM((2, GROUPS, TALL, 128), F32)


def in_vmem(kernel, core, ins, outs, name, cost, aliases={}, scratch=()):
    vmem = pl.BlockSpec(memory_space=pltpu.VMEM)
    return pl.pallas_call(
        kernel,
        in_specs=[pl.BlockSpec(memory_space=pltpu.SMEM)] + [vmem] * len(ins),
        out_specs=[vmem] * len(outs),
        out_shape=outs,
        input_output_aliases={1 + i: o for i, o in aliases.items()},
        scratch_shapes=list(scratch),
        cost_estimate=pl.CostEstimate(flops=int(cost * 1e9), bytes_accessed=int(cost * 3e6), transcendentals=0),
        compiler_params=pltpu.CompilerParams(vmem_limit_bytes=LIMIT),
        name=name,
    )(core, *ins)


def first_section(core, tile, tables):
    def run(outer):
        return lambda *refs: first_kernel(outer, *refs)

    held, strips = [ROWS_SHAPE] * 3, [STRIP_SHAPE] * 2
    *known, inside, outside, start, end = in_vmem(run(True), core, [tile, *tables], held + strips + [EDGE_SHAPE] * 2, "first_outer", 5)
    outer = exchange_x(start, end) + exchange_y(inside, outside)
    *known, inside, outside = in_vmem(run(False), core, [tile, *tables, *known], held + strips, "first_inner", 20, {5: 0, 6: 1, 7: 2})
    return known, outer, exchange_y(inside, outside)


def second_section(core, coef, following, east, outer, inner, tables):
    def run(outer):
        return lambda *refs: middle_kernel(outer, *refs)

    held, strips = [ROWS_SHAPE] * 2, [STRIP_SHAPE] * 2
    shared = [coef, following, east]
    ins = [*shared, *outer[2:], *tables, *outer[:2]]
    *known, inside, outside, start, end = in_vmem(run(True), core, ins, held + strips + [EDGE_SHAPE] * 2, "second_outer", 8, scratch=[STRIPS, SIDE])
    edges = exchange_x(start, end)
    ins = [*shared, *inner, *tables, *known, inside, outside]
    *known, inside, outside = in_vmem(run(False), core, ins, held + [STRIPS_SHAPE] * 2, "second_inner", 20, {9: 0, 10: 1}, [STRIPS])
    return known, edges, exchange_y(inside, outside)


def advanced(core, following, east, edges, strips, scale):
    ins = [following, east, *strips, scale, *edges]
    return in_vmem(last_kernel, core, ins, [PIECES_SHAPE], "advanced", 8, scratch=[ALL_STRIPS, SIDE])[0]


def group_rows(full):
    return slice(REST, MODES) if full else slice(0, REST)


def repeat(count, body):
    lax.fori_loop(0, count, lambda i, _: (body(i), 0)[1], 0)


def pack_kernel(core_ref, state_ref, out_ref):
    row = 1 - core_ref[0]

    def body(s):
        out_ref[s] = state_ref[row, s]

    repeat(SLOTS, body)


def merge_kernel(core_ref, big_ref, state_ref, got_ref, out_ref):
    core = core_ref[0]

    def put(full):
        def body(block):
            out_ref[block, group_rows(full)] = state_ref[core, 0 : SLOTS if full else REST, block]
            out_ref[block, group_rows(not full)] = got_ref[0 : REST if full else SLOTS, block]

        repeat(BLOCKS, body)

    pl.when(core == big_ref[0])(lambda: put(True))
    pl.when(core != big_ref[0])(lambda: put(False))


def split_kernel(own, core_ref, big_ref, pieces_ref, out_ref):
    def get(full):
        slots = SLOTS if full else REST

        def body(block):
            out_ref[0:slots, block] = pieces_ref[block, group_rows(full)]
            if not full:
                out_ref[slots:SLOTS, block] = jnp.zeros((SLOTS - slots, HALVES, 128), F32)

        repeat(BLOCKS, body)

    for full in (False, True):
        pl.when((core_ref[0] == big_ref[0]) == (full == own))(lambda full=full: get(full))


def split_own_kernel(core_ref, big_ref, pieces_ref, out_ref, row, done):
    split_kernel(True, core_ref, big_ref, pieces_ref, row)
    copy = pltpu.make_async_copy(row, out_ref.at[core_ref[0]], done)
    copy.start()
    copy.wait()


def finish_kernel(core_ref, got_ref, _, out_ref, done):
    copy = pltpu.make_async_copy(got_ref, out_ref.at[1 - core_ref[0]], done)
    copy.start()
    copy.wait()


ROW = (SLOTS, BLOCKS, HALVES, 128)
ROW_SHAPE = jax.ShapeDtypeStruct(ROW, F32)
STATE_SHAPE = jax.ShapeDtypeStruct((2, *ROW), F32)
SLOTS_SHAPE = jax.ShapeDtypeStruct((BLOCKS, MODES, HALVES, 128), F32)


def moved(kernel, places, shape, name, aliases={}, scratch=()):
    spec = {"s": pl.BlockSpec(memory_space=pltpu.SMEM), "v": pl.BlockSpec(memory_space=pltpu.VMEM), "a": pl.BlockSpec(memory_space=pl.ANY)}
    return pl.pallas_call(
        kernel,
        in_specs=[spec[p] for p in places[:-1]],
        out_specs=spec[places[-1]],
        out_shape=shape,
        input_output_aliases=aliases,
        scratch_shapes=list(scratch),
        cost_estimate=pl.CostEstimate(flops=int(2e9), bytes_accessed=0, transcendentals=0),
        compiler_params=pltpu.CompilerParams(vmem_limit_bytes=LIMIT),
        name=name,
    )


def to_pieces(core, big, state):
    state = state.reshape(2, SLOTS, FIELDS, 2 * BLOCKS, 128).transpose(0, 1, 3, 2, 4).reshape(2, *ROW)
    got = lax.ppermute(moved(pack_kernel, "svv", ROW_SHAPE, "pack")(core, state), "mode", [(0, 1), (1, 0)])
    return moved(merge_kernel, "ssvvv", SLOTS_SHAPE, "merge")(core, big, state, got)


def from_pieces(core, big, pieces):
    got = lax.ppermute(moved(lambda *refs: split_kernel(False, *refs), "ssvv", ROW_SHAPE, "split_send")(core, big, pieces), "mode", [(0, 1), (1, 0)])
    semaphore = pltpu.SemaphoreType.DMA
    state = moved(split_own_kernel, "ssva", STATE_SHAPE, "split_own", scratch=[pltpu.VMEM(ROW, F32), semaphore])(core, big, pieces)
    state = moved(finish_kernel, "svaa", STATE_SHAPE, "finish", {2: 0}, [semaphore])(core, got, state)
    return state.reshape(2, SLOTS, 2 * BLOCKS, FIELDS, 128).transpose(0, 1, 3, 2, 4).reshape(2, SLOTS, FIELDS, BLOCKS * LANES)


def ring(size, step):
    return [(i, (i + step) % size) for i in range(size)]


def exchange_x(start, end):
    size = lax.axis_size("gx_hi")
    return lax.ppermute(end, "gx_hi", ring(size, 1)), lax.ppermute(start, "gx_hi", ring(size, -1))


def exchange_y(inside, outside):
    place = [(chip * 2 + side) * 2 + core for side in range(2) for chip in range(8) for core in range(2)]
    pairs = [(place[i], place[(i + 1) % 32]) for i in range(1, 32, 2)]
    swap = pairs + [(b, a) for a, b in pairs]
    return lax.ppermute(inside, "mode", [(0, 1), (1, 0)]), lax.ppermute(outside, ("gx_lo", "gy", "mode"), swap)


def shards(chaos_state, mode_group, mode_degrees):
    core = lax.axis_index("mode").astype(jnp.int32).reshape(1)
    evaluate, proj, scale, big = make_tables(mode_group, mode_degrees)
    tables = (evaluate, proj, lane_operators(), scale)
    pieces = to_pieces(core, big, chaos_state)
    tile = lax.all_to_all(pieces.reshape(XROWS, PIECE, 128), ("gx_lo", "mode"), 0, 0, tiled=True)
    (coef, east, following), outer, inner = first_section(core, tile, tables)
    (east, following), edges, strips = second_section(core, coef, following, east, outer, inner, tables)
    tile = advanced(core, following, east, edges, strips, scale)
    pieces = lax.all_to_all(tile, ("gx_lo", "mode"), 0, 0, tiled=True).reshape(SLOTS_SHAPE.shape)
    return from_pieces(core, big, pieces)


def solution(mesh):
    fine = Mesh(mesh.devices.reshape(4, 8, 2, 2), ("gx_hi", "gx_lo", "gy", "mode"))
    spec = P(("gx_hi", "gx_lo"), "mode", None, "gy")
    return jax.shard_map(shards, mesh=fine, in_specs=(spec, P(), P()), out_specs=spec, check_vma=False)
```

```python
import math

import jax
import jax.numpy as jnp
import numpy as np
from jax import lax
from jax.experimental import pallas as pl
from jax.experimental.pallas import tpu as pltpu
from jax.sharding import Mesh, PartitionSpec as P

MODES = 35
FIELDS = 4
QUAD = 81
POINTS = 96
NZ = 16
SLOTS = 24
REST = MODES - SLOTS
SMALL = 16
BLOCKS = 16
HALVES = 2 * FIELDS
PIECE = MODES * HALVES
FULL_AT = REST * HALVES
ROWS = SLOTS + SMALL
LANES = 256
STRIP = 2 * NZ
XROWS = 16
STEP = 4
time_step = 0.05
LIMIT = 10 * 1024 * 1024
F32, BF16 = jnp.float32, jnp.bfloat16


def point_constants():
    p = np.arange(POINTS)
    live = (p < QUAD).astype(np.float64)
    digits = [(p // 3**k) % 3 - 1.0 for k in range(4)]
    xi = [math.sqrt(3.0) * d for d in digits]
    weight = live * np.prod([np.where(d == 0, 4.0, 1.0) for d in digits], axis=0)
    east = 1.2 + 0.5 * xi[0]
    north = 0.6 + 0.5 * xi[1]
    decay = -9.6 * np.exp(0.25 * xi[2])
    rows = np.stack(digits + [weight, east, north, decay]).astype(np.float32)
    cols = np.zeros((POINTS, 8), np.float32)
    cols[:, :4] = np.stack(digits, 1)
    cols[:, 4] = live
    return np.concatenate([rows, rows], axis=1), cols


def degree_factor(n, d):
    square = 3.0 * d * d - 1.0
    cubic = d * d * d - d
    return jnp.where(n == 0.0, 1.0, jnp.where(n == 1.0, d, jnp.where(n == 2.0, square, cubic)))


def degree_norm(n):
    third = 3.0 * math.sqrt(3.0) / math.sqrt(6.0)
    return jnp.where(n == 0.0, 1.0, jnp.where(n == 1.0, math.sqrt(3.0), jnp.where(n == 2.0, 1.0 / math.sqrt(2.0), third)))


def table_kernel(group_ref, degrees_ref, prow_ref, pcol_ref, eval_ref, proj_ref, scale_ref, big_ref):
    sub = lax.broadcasted_iota(jnp.int32, (MODES, MODES), 0)
    lane = lax.broadcasted_iota(jnp.int32, (MODES, MODES), 1)
    grow = group_ref[...].astype(F32)
    gcol = jnp.sum(jnp.where(sub == lane, grow, 0.0), axis=1, keepdims=True)
    degrees = degrees_ref[...].astype(F32)
    degrees_t = [jnp.sum(jnp.where(sub == lane, degrees[:, k : k + 1], 0.0), axis=0, keepdims=True) for k in range(4)]
    big_ref[0] = jnp.where(jnp.sum(grow) == float(SLOTS), 1, 0).astype(jnp.int32)
    same = gcol == grow
    rank_row = jnp.sum(jnp.where(same & (sub < lane), 1.0, 0.0), axis=0, keepdims=True)
    rank_col = jnp.sum(jnp.where(same & (lane < sub), 1.0, 0.0), axis=1, keepdims=True)
    ones = jnp.sum(grow, axis=1, keepdims=True)
    big = jnp.where(ones == float(SLOTS), 1.0, 0.0)
    place_row = jnp.where(grow == big, rank_row, rank_row + SLOTS)
    place_col = jnp.where(gcol == big, rank_col, rank_col + SLOTS)
    row_id = lax.broadcasted_iota(jnp.int32, (ROWS, MODES), 0).astype(F32)
    pick = jnp.where(row_id == place_row, 1.0, 0.0)
    live_col = jnp.sum(pick, axis=1, keepdims=True)
    degree_col = [jnp.sum(pick * degrees_t[k], axis=1, keepdims=True) for k in range(4)]
    lane_id = lax.broadcasted_iota(jnp.int32, (MODES, 128), 1)
    lane_row = jnp.where(lane_id < ROWS, lane_id, jnp.where(lane_id < 2 * ROWS, lane_id - ROWS, lane_id - 2 * ROWS)).astype(F32)
    pick_t = jnp.where(lane_row == place_col, 1.0, 0.0)
    live_row = jnp.sum(pick_t, axis=0, keepdims=True)
    degree_row = [jnp.sum(pick_t * degrees[:, k : k + 1], axis=0, keepdims=True) for k in range(4)]
    basis = live_row * pcol_ref[:, 4:5]
    for k in range(4):
        basis = basis * degree_factor(degree_row[k], pcol_ref[:, k : k + 1])
    projector = live_col * prow_ref[4:5, :]
    scale, inverse = live_col, live_col
    for k in range(4):
        projector = projector * degree_factor(degree_col[k], prow_ref[k : k + 1, :])
        norm = degree_norm(degree_col[k])
        scale = scale * norm
        inverse = inverse / norm
    column = lax.broadcasted_iota(jnp.int32, (1, 128), 1)
    eval_ref[0:POINTS, :] = jnp.where(column < 2 * ROWS, basis, 0.0).astype(BF16)
    linear = []
    for k in range(3):
        left = projector[:, :POINTS] * prow_ref[5 + k : 6 + k, :POINTS]
        full = jnp.dot(left, basis, precision=lax.Precision.HIGHEST, preferred_element_type=F32)
        first = full.astype(BF16).astype(F32)
        linear.append(jnp.where(column < 2 * ROWS, first, jnp.where(column < 3 * ROWS, full - first, 0.0)))
    linear.append(jnp.zeros((8, 128), F32))
    eval_ref[POINTS:, :] = jnp.concatenate(linear, axis=0).astype(BF16)
    proj_ref[...] = jnp.concatenate([projector, projector * prow_ref[3:4, :]], axis=0).astype(BF16)
    scale_ref[0] = jnp.broadcast_to(scale, (ROWS, LANES))
    scale_ref[1] = jnp.broadcast_to(scale * scale * (time_step / (24.0 * 1296.0)), (ROWS, LANES))
    scale_ref[2] = jnp.broadcast_to(inverse, (ROWS, LANES))


def make_tables(mode_group, mode_degrees):
    prow, pcol = point_constants()
    vmem = pl.BlockSpec(memory_space=pltpu.VMEM)
    return pl.pallas_call(
        table_kernel,
        in_specs=[vmem] * 4,
        out_specs=[vmem, vmem, vmem, pl.BlockSpec(memory_space=pltpu.SMEM)],
        out_shape=[
            jax.ShapeDtypeStruct((POINTS + 128, 128), BF16),
            jax.ShapeDtypeStruct((2 * ROWS, 2 * POINTS), BF16),
            jax.ShapeDtypeStruct((3, ROWS, LANES), F32),
            jax.ShapeDtypeStruct((1,), jnp.int32),
        ],
        name="tables",
    )(mode_group[None, :], mode_degrees, jnp.asarray(prow), jnp.asarray(pcol))


def lane_operators():
    source, target = np.meshgrid(np.arange(LANES), np.arange(LANES), indexing="ij")
    gap = source - target
    north = 8.0 * (gap == NZ) - 8.0 * (gap == -NZ) - 1.0 * (gap == 2 * NZ) + 1.0 * (gap == -2 * NZ)
    same_y = source // NZ == target // NZ
    turn = (source - target) % NZ
    laplace = same_y * (1.0 * (turn == 1) + 1.0 * (turn == NZ - 1) - 2.0 * (turn == 0))
    return jnp.asarray(np.stack([np.concatenate([m, m]) for m in (north, laplace)]), BF16)


def pieces_of(value):
    first = value.astype(BF16)
    return first, value - first.astype(F32)


def by_lanes(value, operator):
    first, second = pieces_of(value)
    return first, second, jnp.dot(jnp.concatenate([first, second.astype(BF16)], axis=1), operator, preferred_element_type=F32)


def plane_laplace(value):
    plane = lax.broadcasted_iota(jnp.int32, (1, 128), 1) % NZ
    above = jnp.where(plane == NZ - 1, pltpu.roll(value, NZ - 1, 1), pltpu.roll(value, 127, 1))
    below = jnp.where(plane == 0, pltpu.roll(value, 129 - NZ, 1), pltpu.roll(value, 1, 1))
    return above - 2.0 * value + below


def row_fluxes(fields, eval_ref, proj_ref, lanes_ref):
    points, east, north, source = [], [], [], []
    row = jnp.concatenate(fields, axis=0)
    laplace = jnp.concatenate([plane_laplace(row[:, :128]), plane_laplace(row[:, 128:])], axis=1)
    first, second = pieces_of(row)
    first = first.astype(F32)
    for f in range(FIELDS):
        rows = slice(f * ROWS, (f + 1) * ROWS)
        stack = jnp.concatenate([first[rows], second[rows], first[rows], jnp.zeros((8, LANES), F32)], axis=0).astype(BF16)
        result = jnp.dot(eval_ref[...], stack, preferred_element_type=F32)
        points.append(result[0:POINTS])
        east.append(result[POINTS : POINTS + ROWS])
        north.append(result[POINTS + ROWS : POINTS + 2 * ROWS])
        source.append(result[POINTS + 2 * ROWS : POINTS + 3 * ROWS])

    def project(a, b, both):
        product = points[a] * points[b]
        first, second = pieces_of(product)
        stack = jnp.concatenate([first, second.astype(BF16)], axis=0)
        left = proj_ref[...] if both else proj_ref[0:48, :]
        return jnp.dot(left, stack, preferred_element_type=F32)

    def couple(f, result):
        source[f] = source[f] + (3.6 * result[0:ROWS] + (1.08 * math.sqrt(3.0)) * result[ROWS : 2 * ROWS])

    east[0] = east[0] + project(0, 0, False)[0:ROWS]
    result = project(0, 1, True)
    east[1] = east[1] + result[0:ROWS]
    north[0] = north[0] + result[0:ROWS]
    couple(3, result)
    east[2] = east[2] + project(0, 2, False)[0:ROWS]
    result = project(0, 3, True)
    east[3] = east[3] + result[0:ROWS]
    couple(2, result)
    north[1] = north[1] + project(1, 1, False)[0:ROWS]
    result = project(1, 2, True)
    north[2] = north[2] + result[0:ROWS]
    couple(0, result)
    north[3] = north[3] + project(1, 3, False)[0:ROWS]
    couple(1, project(2, 3, True))
    return east, north, source, laplace


def emit_rows(core_ref, g, at, rows_of, tables, east_ref, next_ref, inside_ref, outside_ref, coef_ref=None):
    eval_ref, proj_ref, lanes_ref, scale_ref = tables
    lane = lax.broadcasted_iota(jnp.int32, (1, 128), 1)
    gain = scale_ref[1]
    low, high = [None] * FIELDS, [None] * FIELDS
    given = [rows_of(r) for r in range(STEP)]
    found = []
    for fields, base, weight in given:
        east, north, source, laplace = row_fluxes(fields, eval_ref, proj_ref, lanes_ref)
        slope = by_lanes(jnp.concatenate(north, axis=0), lanes_ref[0])[2]
        following = []
        for f in range(FIELDS):
            rows = slice(f * ROWS, (f + 1) * ROWS)
            known = gain * (source[f] - slope[rows]) + time_step * laplace[rows]
            following.append(base[f] + weight * known)
        found.append((east, north, following))
    for r in range(STEP):
        east, north, following = found[r]
        here = (lane >= r * STRIP) & (lane < (r + 1) * STRIP)
        for f in range(FIELDS):
            rows = slice(f * ROWS, (f + 1) * ROWS)
            if coef_ref is not None:
                coef_ref[STEP * g + r, rows, :] = given[r][0][f]
            east_ref[STEP * g + r, rows, :] = east[f]
            next_ref[STEP * g + r, rows, :] = following[f]
            start = pltpu.roll(north[f][:, :128], r * STRIP, 1) if r else north[f][:, :128]
            end = north[f][:, 128:] if r == STEP - 1 else pltpu.roll(north[f][:, 128:], (r + 1) * STRIP, 1)
            low[f] = jnp.where(here, start, low[f]) if r else start
            high[f] = jnp.where(here, end, high[f]) if r else end

    def store(inside, outside):
        for f in range(FIELDS):
            inside_ref[at, f * ROWS : (f + 1) * ROWS, :] = inside[f]
            outside_ref[at, f * ROWS : (f + 1) * ROWS, :] = outside[f]

    pl.when(core_ref[0] == 0)(lambda: store(high, low))
    pl.when(core_ref[0] == 1)(lambda: store(low, high))


def from_neighbours(i, r, f, row, strips):
    rows = slice(f * ROWS, (f + 1) * ROWS)
    total = 8.0 * (row(r + 1, rows) - row(r - 1, rows)) - (row(r + 2, rows) - row(r - 2, rows))
    lane = lax.broadcasted_iota(jnp.int32, (1, 128), 1)
    below, above = strips[0, i, rows, :], strips[1, i, rows, :]
    if r:
        below = pltpu.roll(below, 128 - r * STRIP, 1)
    if r != STEP - 1:
        above = pltpu.roll(above, 96 - r * STRIP, 1)
    low = jnp.where(lane < STRIP, below, 0.0) - jnp.where(lane < NZ, 8.0, 0.0) * pltpu.roll(below, 128 - NZ, 1)
    high = jnp.where(lane >= 128 - NZ, 8.0, 0.0) * pltpu.roll(above, NZ, 1) - jnp.where(lane >= 128 - STRIP, above, 0.0)
    return total + jnp.concatenate([low, high], axis=1)


GROUPS = XROWS // STEP


def over_groups(outer, body):
    lax.fori_loop(0, 2, lambda i, _: (body((GROUPS - 1) * i if outer else 1 + i, i), 0)[1], 0)


def edges_of(east_ref, start_ref, end_ref):
    for k in range(2):
        start_ref[k] = east_ref[k]
        end_ref[k] = east_ref[XROWS - 2 + k]


def first_kernel(outer, core_ref, *refs):
    state_ref, tables = refs[0], refs[1:5]
    coef_ref, east_ref, next_ref, inside_ref, outside_ref = refs[5:10] if outer else refs[8:13]

    def body(g, i):
        def rows_of(r):
            fields = []
            for f in range(FIELDS):
                halves = []
                for half in range(2):
                    full = state_ref[STEP * g + r, pl.ds(FULL_AT + half * FIELDS + f, SLOTS, stride=HALVES), :]
                    rest = state_ref[STEP * g + r, pl.ds(half * FIELDS + f, SMALL, stride=HALVES), :]
                    halves.append(jnp.concatenate([full, rest], axis=0))
                value = tables[3][0] * jnp.concatenate(halves, axis=1)
                fields.append(value)
            return fields, fields, 1.0

        emit_rows(core_ref, g, i, rows_of, tables, east_ref, next_ref, inside_ref, outside_ref, coef_ref)

    over_groups(outer, body)
    if outer:
        edges_of(east_ref, *refs[10:12])


def neighbour_strips(core_ref, inside_ref, outside_ref, strips):
    def hold(below_ref, above_ref):
        strips[0] = below_ref[...]
        strips[1] = above_ref[...]

    pl.when(core_ref[0] == 0)(lambda: hold(outside_ref, inside_ref))
    pl.when(core_ref[0] == 1)(lambda: hold(inside_ref, outside_ref))


def side_rows(outer, east_ref, edge_before, edge_after, side_ref):
    if outer:
        side_ref[0, 0:2] = edge_before[...]
        side_ref[0, 2:4] = east_ref[STEP : STEP + 2]
        side_ref[1, 0:2] = east_ref[XROWS - STEP - 2 : XROWS - STEP]
        side_ref[1, 2:4] = edge_after[...]

    def row_at(g, i):
        def row(k, rows):
            if outer and k < 0:
                return side_ref[i, k + 2, rows, :]
            if outer and k >= STEP:
                return side_ref[i, k - STEP + 2, rows, :]
            return east_ref[STEP * g + k, rows, :]

        return row

    return row_at


def middle_kernel(outer, core_ref, *refs):
    coef_ref, following_ref, from_ref, inside_from, outside_from = refs[:5]
    tables = refs[5:9]
    if outer:
        edges, (east_ref, next_ref, inside_ref, outside_ref), ends, (strips, side) = refs[9:11], refs[11:15], refs[15:17], refs[17:]
    else:
        edges, (east_ref, next_ref, inside_ref, outside_ref), ends, (strips, side) = (None, None), refs[13:17], None, (refs[17], None)
        for given, held in ((refs[11], inside_ref), (refs[12], outside_ref)):
            held[0] = given[0]
            held[GROUPS - 1] = given[1]
    row_at = side_rows(outer, from_ref, *edges, side)
    neighbour_strips(core_ref, inside_from, outside_from, strips)

    def body(g, i):
        def rows_of(r):
            section, base = [], []
            for f in range(FIELDS):
                rows = slice(f * ROWS, (f + 1) * ROWS)
                missing = from_neighbours(i, r, f, row_at(g, i), strips)
                section.append(following_ref[STEP * g + r, rows, :] - tables[3][1] * missing)
                base.append(0.5 * (coef_ref[STEP * g + r, rows, :] + section[f]))
            return section, base, 0.5

        emit_rows(core_ref, g, i if outer else g, rows_of, tables, east_ref, next_ref, inside_ref, outside_ref)

    over_groups(outer, body)
    if outer:
        edges_of(east_ref, *ends)


def last_kernel(core_ref, following_ref, from_ref, inside_from, outside_from, scale_ref, edge_before, edge_after, state_ref, strips, side):
    neighbour_strips(core_ref, inside_from, outside_from, strips)
    for outer in (True, False):
        row_at = side_rows(outer, from_ref, edge_before, edge_after, side)

        def body(g, i):
            for r in range(STEP):
                for f in range(FIELDS):
                    rows = slice(f * ROWS, (f + 1) * ROWS)
                    missing = from_neighbours(g, r, f, row_at(g, i), strips)
                    value = scale_ref[2] * (following_ref[STEP * g + r, rows, :] - 0.5 * scale_ref[1] * missing)
                    for half in range(2):
                        lanes = slice(half * 128, (half + 1) * 128)
                        state_ref[STEP * g + r, pl.ds(FULL_AT + half * FIELDS + f, SLOTS, stride=HALVES), :] = value[:SLOTS, lanes]
                        state_ref[STEP * g + r, pl.ds(half * FIELDS + f, REST, stride=HALVES), :] = value[SLOTS:MODES, lanes]

        over_groups(outer, body)


TALL = FIELDS * ROWS
ROWS_SHAPE = jax.ShapeDtypeStruct((XROWS, TALL, LANES), F32)
EDGE_SHAPE = jax.ShapeDtypeStruct((2, TALL, LANES), F32)
STRIP_SHAPE = jax.ShapeDtypeStruct((2, TALL, 128), F32)
STRIPS_SHAPE = jax.ShapeDtypeStruct((GROUPS, TALL, 128), F32)
PIECES_SHAPE = jax.ShapeDtypeStruct((XROWS, PIECE, 128), F32)
SIDE = pltpu.VMEM((2, 4, TALL, LANES), F32)
STRIPS = pltpu.VMEM((2, 2, TALL, 128), F32)
ALL_STRIPS = pltpu.VMEM((2, GROUPS, TALL, 128), F32)


def in_vmem(kernel, core, ins, outs, name, cost, aliases={}, scratch=()):
    vmem = pl.BlockSpec(memory_space=pltpu.VMEM)
    return pl.pallas_call(
        kernel,
        in_specs=[pl.BlockSpec(memory_space=pltpu.SMEM)] + [vmem] * len(ins),
        out_specs=[vmem] * len(outs),
        out_shape=outs,
        input_output_aliases={1 + i: o for i, o in aliases.items()},
        scratch_shapes=list(scratch),
        cost_estimate=pl.CostEstimate(flops=int(cost * 1e9), bytes_accessed=int(cost * 3e6), transcendentals=0),
        compiler_params=pltpu.CompilerParams(vmem_limit_bytes=LIMIT),
        name=name,
    )(core, *ins)


def first_section(core, tile, tables):
    def run(outer):
        return lambda *refs: first_kernel(outer, *refs)

    held, strips = [ROWS_SHAPE] * 3, [STRIP_SHAPE] * 2
    *known, inside, outside, start, end = in_vmem(run(True), core, [tile, *tables], held + strips + [EDGE_SHAPE] * 2, "first_outer", 5)
    outer = exchange_x(start, end) + exchange_y(inside, outside)
    *known, inside, outside = in_vmem(run(False), core, [tile, *tables, *known], held + strips, "first_inner", 20, {5: 0, 6: 1, 7: 2})
    return known, outer, exchange_y(inside, outside)


def second_section(core, coef, following, east, outer, inner, tables):
    def run(outer):
        return lambda *refs: middle_kernel(outer, *refs)

    held, strips = [ROWS_SHAPE] * 2, [STRIP_SHAPE] * 2
    shared = [coef, following, east]
    ins = [*shared, *outer[2:], *tables, *outer[:2]]
    *known, inside, outside, start, end = in_vmem(run(True), core, ins, held + strips + [EDGE_SHAPE] * 2, "second_outer", 8, scratch=[STRIPS, SIDE])
    edges = exchange_x(start, end)
    ins = [*shared, *inner, *tables, *known, inside, outside]
    *known, inside, outside = in_vmem(run(False), core, ins, held + [STRIPS_SHAPE] * 2, "second_inner", 20, {9: 0, 10: 1}, [STRIPS])
    return known, edges, exchange_y(inside, outside)


def advanced(core, following, east, edges, strips, scale):
    ins = [following, east, *strips, scale, *edges]
    return in_vmem(last_kernel, core, ins, [PIECES_SHAPE], "advanced", 8, scratch=[ALL_STRIPS, SIDE])[0]


def group_rows(full):
    return slice(REST, MODES) if full else slice(0, REST)


def repeat(count, body):
    lax.fori_loop(0, count, lambda i, _: (body(i), 0)[1], 0)


def pack_kernel(core_ref, state_ref, out_ref):
    row = 1 - core_ref[0]

    def body(s):
        out_ref[s] = state_ref[row, s]

    repeat(SLOTS, body)


def merge_kernel(core_ref, big_ref, state_ref, got_ref, out_ref):
    core = core_ref[0]

    def put(full):
        def body(block):
            out_ref[block, group_rows(full)] = state_ref[core, 0 : SLOTS if full else REST, block]
            out_ref[block, group_rows(not full)] = got_ref[0 : REST if full else SLOTS, block]

        repeat(BLOCKS, body)

    pl.when(core == big_ref[0])(lambda: put(True))
    pl.when(core != big_ref[0])(lambda: put(False))


def split_kernel(own, core_ref, big_ref, pieces_ref, out_ref):
    def get(full):
        slots = SLOTS if full else REST

        def body(block):
            out_ref[0:slots, block] = pieces_ref[block, group_rows(full)]
            if not full:
                out_ref[slots:SLOTS, block] = jnp.zeros((SLOTS - slots, HALVES, 128), F32)

        repeat(BLOCKS, body)

    for full in (False, True):
        pl.when((core_ref[0] == big_ref[0]) == (full == own))(lambda full=full: get(full))


def split_own_kernel(core_ref, big_ref, pieces_ref, out_ref, row, done):
    split_kernel(True, core_ref, big_ref, pieces_ref, row)
    copy = pltpu.make_async_copy(row, out_ref.at[core_ref[0]], done)
    copy.start()
    copy.wait()


def finish_kernel(core_ref, got_ref, _, out_ref, done):
    copy = pltpu.make_async_copy(got_ref, out_ref.at[1 - core_ref[0]], done)
    copy.start()
    copy.wait()


ROW = (SLOTS, BLOCKS, HALVES, 128)
ROW_SHAPE = jax.ShapeDtypeStruct(ROW, F32)
STATE_SHAPE = jax.ShapeDtypeStruct((2, *ROW), F32)
SLOTS_SHAPE = jax.ShapeDtypeStruct((BLOCKS, MODES, HALVES, 128), F32)


def moved(kernel, places, shape, name, aliases={}, scratch=()):
    spec = {"s": pl.BlockSpec(memory_space=pltpu.SMEM), "v": pl.BlockSpec(memory_space=pltpu.VMEM), "a": pl.BlockSpec(memory_space=pl.ANY)}
    return pl.pallas_call(
        kernel,
        in_specs=[spec[p] for p in places[:-1]],
        out_specs=spec[places[-1]],
        out_shape=shape,
        input_output_aliases=aliases,
        scratch_shapes=list(scratch),
        cost_estimate=pl.CostEstimate(flops=int(2e9), bytes_accessed=0, transcendentals=0),
        compiler_params=pltpu.CompilerParams(vmem_limit_bytes=LIMIT),
        name=name,
    )


def to_pieces(core, big, state):
    state = state.reshape(2, SLOTS, FIELDS, 2 * BLOCKS, 128).transpose(0, 1, 3, 2, 4).reshape(2, *ROW)
    got = lax.ppermute(moved(pack_kernel, "svv", ROW_SHAPE, "pack")(core, state), "mode", [(0, 1), (1, 0)])
    return moved(merge_kernel, "ssvvv", SLOTS_SHAPE, "merge")(core, big, state, got)


def from_pieces(core, big, pieces):
    got = lax.ppermute(moved(lambda *refs: split_kernel(False, *refs), "ssvv", ROW_SHAPE, "split_send")(core, big, pieces), "mode", [(0, 1), (1, 0)])
    semaphore = pltpu.SemaphoreType.DMA
    state = moved(split_own_kernel, "ssva", STATE_SHAPE, "split_own", scratch=[pltpu.VMEM(ROW, F32), semaphore])(core, big, pieces)
    state = moved(finish_kernel, "svaa", STATE_SHAPE, "finish", {2: 0}, [semaphore])(core, got, state)
    return state.reshape(2, SLOTS, 2 * BLOCKS, FIELDS, 128).transpose(0, 1, 3, 2, 4).reshape(2, SLOTS, FIELDS, BLOCKS * LANES)


def ring(size, step):
    return [(i, (i + step) % size) for i in range(size)]


def exchange_x(start, end):
    size = lax.axis_size("gx_hi")
    return lax.ppermute(end, "gx_hi", ring(size, 1)), lax.ppermute(start, "gx_hi", ring(size, -1))


def exchange_y(inside, outside):
    place = [(chip * 2 + side) * 2 + core for side in range(2) for chip in range(8) for core in range(2)]
    pairs = [(place[i], place[(i + 1) % 32]) for i in range(1, 32, 2)]
    swap = pairs + [(b, a) for a, b in pairs]
    return lax.ppermute(inside, "mode", [(0, 1), (1, 0)]), lax.ppermute(outside, ("gx_lo", "gy", "mode"), swap)


def shards(chaos_state, mode_group, mode_degrees):
    core = lax.axis_index("mode").astype(jnp.int32).reshape(1)
    evaluate, proj, scale, big = make_tables(mode_group, mode_degrees)
    tables = (evaluate, proj, lane_operators(), scale)
    pieces = to_pieces(core, big, chaos_state)
    tile = lax.all_to_all(pieces.reshape(XROWS, PIECE, 128), ("gx_lo", "mode"), 0, 0, tiled=True)
    (coef, east, following), outer, inner = first_section(core, tile, tables)
    (east, following), edges, strips = second_section(core, coef, following, east, outer, inner, tables)
    tile = advanced(core, following, east, edges, strips, scale)
    pieces = lax.all_to_all(tile, ("gx_lo", "mode"), 0, 0, tiled=True).reshape(SLOTS_SHAPE.shape)
    return from_pieces(core, big, pieces)


def solution(mesh):
    fine = Mesh(mesh.devices.reshape(4, 8, 2, 2), ("gx_hi", "gx_lo", "gy", "mode"))
    spec = P(("gx_hi", "gx_lo"), "mode", None, "gy")
    return jax.shard_map(shards, mesh=fine, in_specs=(spec, P(), P()), out_specs=spec, check_vma=False)
```

```python
import math

import jax
import jax.numpy as jnp
import numpy as np
from jax import lax
from jax.experimental import pallas as pl
from jax.experimental.pallas import tpu as pltpu
from jax.sharding import Mesh, PartitionSpec as P

MODES = 35
FIELDS = 4
QUAD = 81
POINTS = 96
NZ = 16
SLOTS = 24
REST = MODES - SLOTS
SMALL = 16
BLOCKS = 16
HALVES = 2 * FIELDS
PIECE = MODES * HALVES
FULL_AT = REST * HALVES
ROWS = SLOTS + SMALL
LANES = 256
STRIP = 2 * NZ
XROWS = 16
STEP = 4
time_step = 0.05
LIMIT = 10 * 1024 * 1024
F32, BF16 = jnp.float32, jnp.bfloat16


def point_constants():
    p = np.arange(POINTS)
    live = (p < QUAD).astype(np.float64)
    digits = [(p // 3**k) % 3 - 1.0 for k in range(4)]
    xi = [math.sqrt(3.0) * d for d in digits]
    weight = live * np.prod([np.where(d == 0, 4.0, 1.0) for d in digits], axis=0)
    east = 1.2 + 0.5 * xi[0]
    north = 0.6 + 0.5 * xi[1]
    decay = -9.6 * np.exp(0.25 * xi[2])
    rows = np.stack(digits + [weight, east, north, decay]).astype(np.float32)
    cols = np.zeros((POINTS, 8), np.float32)
    cols[:, :4] = np.stack(digits, 1)
    cols[:, 4] = live
    return np.concatenate([rows, rows], axis=1), cols


def degree_factor(n, d):
    square = 3.0 * d * d - 1.0
    cubic = d * d * d - d
    return jnp.where(n == 0.0, 1.0, jnp.where(n == 1.0, d, jnp.where(n == 2.0, square, cubic)))


def degree_norm(n):
    third = 3.0 * math.sqrt(3.0) / math.sqrt(6.0)
    return jnp.where(n == 0.0, 1.0, jnp.where(n == 1.0, math.sqrt(3.0), jnp.where(n == 2.0, 1.0 / math.sqrt(2.0), third)))


def table_kernel(group_ref, degrees_ref, prow_ref, pcol_ref, eval_ref, proj_ref, scale_ref, big_ref):
    sub = lax.broadcasted_iota(jnp.int32, (MODES, MODES), 0)
    lane = lax.broadcasted_iota(jnp.int32, (MODES, MODES), 1)
    grow = group_ref[...].astype(F32)
    gcol = jnp.sum(jnp.where(sub == lane, grow, 0.0), axis=1, keepdims=True)
    degrees = degrees_ref[...].astype(F32)
    degrees_t = [jnp.sum(jnp.where(sub == lane, degrees[:, k : k + 1], 0.0), axis=0, keepdims=True) for k in range(4)]
    big_ref[0] = jnp.where(jnp.sum(grow) == float(SLOTS), 1, 0).astype(jnp.int32)
    same = gcol == grow
    rank_row = jnp.sum(jnp.where(same & (sub < lane), 1.0, 0.0), axis=0, keepdims=True)
    rank_col = jnp.sum(jnp.where(same & (lane < sub), 1.0, 0.0), axis=1, keepdims=True)
    ones = jnp.sum(grow, axis=1, keepdims=True)
    big = jnp.where(ones == float(SLOTS), 1.0, 0.0)
    place_row = jnp.where(grow == big, rank_row, rank_row + SLOTS)
    place_col = jnp.where(gcol == big, rank_col, rank_col + SLOTS)
    row_id = lax.broadcasted_iota(jnp.int32, (ROWS, MODES), 0).astype(F32)
    pick = jnp.where(row_id == place_row, 1.0, 0.0)
    live_col = jnp.sum(pick, axis=1, keepdims=True)
    degree_col = [jnp.sum(pick * degrees_t[k], axis=1, keepdims=True) for k in range(4)]
    lane_id = lax.broadcasted_iota(jnp.int32, (MODES, 128), 1)
    lane_row = jnp.where(lane_id < ROWS, lane_id, jnp.where(lane_id < 2 * ROWS, lane_id - ROWS, lane_id - 2 * ROWS)).astype(F32)
    pick_t = jnp.where(lane_row == place_col, 1.0, 0.0)
    live_row = jnp.sum(pick_t, axis=0, keepdims=True)
    degree_row = [jnp.sum(pick_t * degrees[:, k : k + 1], axis=0, keepdims=True) for k in range(4)]
    basis = live_row * pcol_ref[:, 4:5]
    for k in range(4):
        basis = basis * degree_factor(degree_row[k], pcol_ref[:, k : k + 1])
    projector = live_col * prow_ref[4:5, :]
    scale, inverse = live_col, live_col
    for k in range(4):
        projector = projector * degree_factor(degree_col[k], prow_ref[k : k + 1, :])
        norm = degree_norm(degree_col[k])
        scale = scale * norm
        inverse = inverse / norm
    column = lax.broadcasted_iota(jnp.int32, (1, 128), 1)
    eval_ref[0:POINTS, :] = jnp.where(column < 2 * ROWS, basis, 0.0).astype(BF16)
    linear = []
    for k in range(3):
        left = projector[:, :POINTS] * prow_ref[5 + k : 6 + k, :POINTS]
        full = jnp.dot(left, basis, precision=lax.Precision.HIGHEST, preferred_element_type=F32)
        first = full.astype(BF16).astype(F32)
        linear.append(jnp.where(column < 2 * ROWS, first, jnp.where(column < 3 * ROWS, full - first, 0.0)))
    linear.append(jnp.zeros((8, 128), F32))
    eval_ref[POINTS:, :] = jnp.concatenate(linear, axis=0).astype(BF16)
    proj_ref[...] = jnp.concatenate([projector, projector * prow_ref[3:4, :]], axis=0).astype(BF16)
    scale_ref[0] = jnp.broadcast_to(scale, (ROWS, LANES))
    scale_ref[1] = jnp.broadcast_to(scale * scale * (time_step / (24.0 * 1296.0)), (ROWS, LANES))
    scale_ref[2] = jnp.broadcast_to(inverse, (ROWS, LANES))


def make_tables(mode_group, mode_degrees):
    prow, pcol = point_constants()
    vmem = pl.BlockSpec(memory_space=pltpu.VMEM)
    return pl.pallas_call(
        table_kernel,
        in_specs=[vmem] * 4,
        out_specs=[vmem, vmem, vmem, pl.BlockSpec(memory_space=pltpu.SMEM)],
        out_shape=[
            jax.ShapeDtypeStruct((POINTS + 128, 128), BF16),
            jax.ShapeDtypeStruct((2 * ROWS, 2 * POINTS), BF16),
            jax.ShapeDtypeStruct((3, ROWS, LANES), F32),
            jax.ShapeDtypeStruct((1,), jnp.int32),
        ],
        name="tables",
    )(mode_group[None, :], mode_degrees, jnp.asarray(prow), jnp.asarray(pcol))


def lane_operators():
    source, target = np.meshgrid(np.arange(LANES), np.arange(LANES), indexing="ij")
    gap = source - target
    north = 8.0 * (gap == NZ) - 8.0 * (gap == -NZ) - 1.0 * (gap == 2 * NZ) + 1.0 * (gap == -2 * NZ)
    same_y = source // NZ == target // NZ
    turn = (source - target) % NZ
    laplace = same_y * (1.0 * (turn == 1) + 1.0 * (turn == NZ - 1) - 2.0 * (turn == 0))
    return jnp.asarray(np.stack([np.concatenate([m, m]) for m in (north, laplace)]), BF16)


def pieces_of(value):
    first = value.astype(BF16)
    return first, value - first.astype(F32)


def by_lanes(value, operator):
    first, second = pieces_of(value)
    return first, second, jnp.dot(jnp.concatenate([first, second.astype(BF16)], axis=1), operator, preferred_element_type=F32)


def row_fluxes(fields, eval_ref, proj_ref, lanes_ref):
    points, east, north, source = [], [], [], []
    first, second, laplace = by_lanes(jnp.concatenate(fields, axis=0), lanes_ref[1])
    first = first.astype(F32)
    for f in range(FIELDS):
        rows = slice(f * ROWS, (f + 1) * ROWS)
        stack = jnp.concatenate([first[rows], second[rows], first[rows], jnp.zeros((8, LANES), F32)], axis=0).astype(BF16)
        result = jnp.dot(eval_ref[...], stack, preferred_element_type=F32)
        points.append(result[0:POINTS])
        east.append(result[POINTS : POINTS + ROWS])
        north.append(result[POINTS + ROWS : POINTS + 2 * ROWS])
        source.append(result[POINTS + 2 * ROWS : POINTS + 3 * ROWS])

    def project(a, b, both):
        product = points[a] * points[b]
        first, second = pieces_of(product)
        stack = jnp.concatenate([first, second.astype(BF16)], axis=0)
        left = proj_ref[...] if both else proj_ref[0:48, :]
        return jnp.dot(left, stack, preferred_element_type=F32)

    def couple(f, result):
        source[f] = source[f] + (3.6 * result[0:ROWS] + (1.08 * math.sqrt(3.0)) * result[ROWS : 2 * ROWS])

    east[0] = east[0] + project(0, 0, False)[0:ROWS]
    result = project(0, 1, True)
    east[1] = east[1] + result[0:ROWS]
    north[0] = north[0] + result[0:ROWS]
    couple(3, result)
    east[2] = east[2] + project(0, 2, False)[0:ROWS]
    result = project(0, 3, True)
    east[3] = east[3] + result[0:ROWS]
    couple(2, result)
    north[1] = north[1] + project(1, 1, False)[0:ROWS]
    result = project(1, 2, True)
    north[2] = north[2] + result[0:ROWS]
    couple(0, result)
    north[3] = north[3] + project(1, 3, False)[0:ROWS]
    couple(1, project(2, 3, True))
    return east, north, source, laplace


def emit_rows(core_ref, g, at, rows_of, tables, east_ref, next_ref, inside_ref, outside_ref):
    eval_ref, proj_ref, lanes_ref, scale_ref = tables
    lane = lax.broadcasted_iota(jnp.int32, (1, 128), 1)
    gain = scale_ref[1]
    low, high = [None] * FIELDS, [None] * FIELDS
    for r in range(STEP):
        fields, base, weight = rows_of(r)
        east, north, source, laplace = row_fluxes(fields, eval_ref, proj_ref, lanes_ref)
        here = (lane >= r * STRIP) & (lane < (r + 1) * STRIP)
        slope = by_lanes(jnp.concatenate(north, axis=0), lanes_ref[0])[2]
        for f in range(FIELDS):
            rows = slice(f * ROWS, (f + 1) * ROWS)
            east_ref[STEP * g + r, rows, :] = east[f]
            known = gain * (source[f] - slope[rows]) + time_step * laplace[rows]
            next_ref[STEP * g + r, rows, :] = base[f] + weight * known
            start = pltpu.roll(north[f][:, :128], r * STRIP, 1) if r else north[f][:, :128]
            end = north[f][:, 128:] if r == STEP - 1 else pltpu.roll(north[f][:, 128:], (r + 1) * STRIP, 1)
            low[f] = jnp.where(here, start, low[f]) if r else start
            high[f] = jnp.where(here, end, high[f]) if r else end

    def store(inside, outside):
        for f in range(FIELDS):
            inside_ref[at, f * ROWS : (f + 1) * ROWS, :] = inside[f]
            outside_ref[at, f * ROWS : (f + 1) * ROWS, :] = outside[f]

    pl.when(core_ref[0] == 0)(lambda: store(high, low))
    pl.when(core_ref[0] == 1)(lambda: store(low, high))


def from_neighbours(i, r, f, row, strips):
    rows = slice(f * ROWS, (f + 1) * ROWS)
    total = 8.0 * (row(r + 1, rows) - row(r - 1, rows)) - (row(r + 2, rows) - row(r - 2, rows))
    lane = lax.broadcasted_iota(jnp.int32, (1, 128), 1)
    below, above = strips[0, i, rows, :], strips[1, i, rows, :]
    if r:
        below = pltpu.roll(below, 128 - r * STRIP, 1)
    if r != STEP - 1:
        above = pltpu.roll(above, 96 - r * STRIP, 1)
    low = jnp.where(lane < STRIP, below, 0.0) - jnp.where(lane < NZ, 8.0, 0.0) * pltpu.roll(below, 128 - NZ, 1)
    high = jnp.where(lane >= 128 - NZ, 8.0, 0.0) * pltpu.roll(above, NZ, 1) - jnp.where(lane >= 128 - STRIP, above, 0.0)
    return total + jnp.concatenate([low, high], axis=1)


GROUPS = XROWS // STEP


def over_groups(outer, body):
    lax.fori_loop(0, 2, lambda i, _: (body((GROUPS - 1) * i if outer else 1 + i, i), 0)[1], 0)


def edges_of(east_ref, start_ref, end_ref):
    for k in range(2):
        start_ref[k] = east_ref[k]
        end_ref[k] = east_ref[XROWS - 2 + k]


def first_kernel(outer, core_ref, *refs):
    state_ref, tables = refs[0], refs[1:5]
    coef_ref, east_ref, next_ref, inside_ref, outside_ref = refs[5:10] if outer else refs[8:13]

    def body(g, i):
        def rows_of(r):
            fields = []
            for f in range(FIELDS):
                halves = []
                for half in range(2):
                    full = state_ref[STEP * g + r, pl.ds(FULL_AT + half * FIELDS + f, SLOTS, stride=HALVES), :]
                    rest = state_ref[STEP * g + r, pl.ds(half * FIELDS + f, SMALL, stride=HALVES), :]
                    halves.append(jnp.concatenate([full, rest], axis=0))
                value = tables[3][0] * jnp.concatenate(halves, axis=1)
                coef_ref[STEP * g + r, f * ROWS : (f + 1) * ROWS, :] = value
                fields.append(value)
            return fields, fields, 1.0

        emit_rows(core_ref, g, i, rows_of, tables, east_ref, next_ref, inside_ref, outside_ref)

    over_groups(outer, body)
    if outer:
        edges_of(east_ref, *refs[10:12])


def neighbour_strips(core_ref, inside_ref, outside_ref, strips):
    def hold(below_ref, above_ref):
        strips[0] = below_ref[...]
        strips[1] = above_ref[...]

    pl.when(core_ref[0] == 0)(lambda: hold(outside_ref, inside_ref))
    pl.when(core_ref[0] == 1)(lambda: hold(inside_ref, outside_ref))


def side_rows(outer, east_ref, edge_before, edge_after, side_ref):
    if outer:
        side_ref[0, 0:2] = edge_before[...]
        side_ref[0, 2:4] = east_ref[STEP : STEP + 2]
        side_ref[1, 0:2] = east_ref[XROWS - STEP - 2 : XROWS - STEP]
        side_ref[1, 2:4] = edge_after[...]

    def row_at(g, i):
        def row(k, rows):
            if outer and k < 0:
                return side_ref[i, k + 2, rows, :]
            if outer and k >= STEP:
                return side_ref[i, k - STEP + 2, rows, :]
            return east_ref[STEP * g + k, rows, :]

        return row

    return row_at


def middle_kernel(outer, core_ref, *refs):
    coef_ref, following_ref, from_ref, inside_from, outside_from = refs[:5]
    tables = refs[5:9]
    if outer:
        edges, (east_ref, next_ref, inside_ref, outside_ref), ends, (strips, side) = refs[9:11], refs[11:15], refs[15:17], refs[17:]
    else:
        edges, (east_ref, next_ref, inside_ref, outside_ref), ends, (strips, side) = (None, None), refs[13:17], None, (refs[17], None)
        for given, held in ((refs[11], inside_ref), (refs[12], outside_ref)):
            held[0] = given[0]
            held[GROUPS - 1] = given[1]
    row_at = side_rows(outer, from_ref, *edges, side)
    neighbour_strips(core_ref, inside_from, outside_from, strips)

    def body(g, i):
        def rows_of(r):
            section, base = [], []
            for f in range(FIELDS):
                rows = slice(f * ROWS, (f + 1) * ROWS)
                missing = from_neighbours(i, r, f, row_at(g, i), strips)
                section.append(following_ref[STEP * g + r, rows, :] - tables[3][1] * missing)
                base.append(0.5 * (coef_ref[STEP * g + r, rows, :] + section[f]))
            return section, base, 0.5

        emit_rows(core_ref, g, i if outer else g, rows_of, tables, east_ref, next_ref, inside_ref, outside_ref)

    over_groups(outer, body)
    if outer:
        edges_of(east_ref, *ends)


def last_kernel(core_ref, following_ref, from_ref, inside_from, outside_from, scale_ref, edge_before, edge_after, state_ref, strips, side):
    neighbour_strips(core_ref, inside_from, outside_from, strips)
    for outer in (True, False):
        row_at = side_rows(outer, from_ref, edge_before, edge_after, side)

        def body(g, i):
            for r in range(STEP):
                for f in range(FIELDS):
                    rows = slice(f * ROWS, (f + 1) * ROWS)
                    missing = from_neighbours(g, r, f, row_at(g, i), strips)
                    value = scale_ref[2] * (following_ref[STEP * g + r, rows, :] - 0.5 * scale_ref[1] * missing)
                    for half in range(2):
                        lanes = slice(half * 128, (half + 1) * 128)
                        state_ref[STEP * g + r, pl.ds(FULL_AT + half * FIELDS + f, SLOTS, stride=HALVES), :] = value[:SLOTS, lanes]
                        state_ref[STEP * g + r, pl.ds(half * FIELDS + f, REST, stride=HALVES), :] = value[SLOTS:MODES, lanes]

        over_groups(outer, body)


TALL = FIELDS * ROWS
ROWS_SHAPE = jax.ShapeDtypeStruct((XROWS, TALL, LANES), F32)
EDGE_SHAPE = jax.ShapeDtypeStruct((2, TALL, LANES), F32)
STRIP_SHAPE = jax.ShapeDtypeStruct((2, TALL, 128), F32)
STRIPS_SHAPE = jax.ShapeDtypeStruct((GROUPS, TALL, 128), F32)
PIECES_SHAPE = jax.ShapeDtypeStruct((XROWS, PIECE, 128), F32)
SIDE = pltpu.VMEM((2, 4, TALL, LANES), F32)
STRIPS = pltpu.VMEM((2, 2, TALL, 128), F32)
ALL_STRIPS = pltpu.VMEM((2, GROUPS, TALL, 128), F32)


def in_vmem(kernel, core, ins, outs, name, cost, aliases={}, scratch=()):
    vmem = pl.BlockSpec(memory_space=pltpu.VMEM)
    return pl.pallas_call(
        kernel,
        in_specs=[pl.BlockSpec(memory_space=pltpu.SMEM)] + [vmem] * len(ins),
        out_specs=[vmem] * len(outs),
        out_shape=outs,
        input_output_aliases={1 + i: o for i, o in aliases.items()},
        scratch_shapes=list(scratch),
        cost_estimate=pl.CostEstimate(flops=int(cost * 1e9), bytes_accessed=int(cost * 3e6), transcendentals=0),
        compiler_params=pltpu.CompilerParams(vmem_limit_bytes=LIMIT),
        name=name,
    )(core, *ins)


def first_section(core, tile, tables):
    def run(outer):
        return lambda *refs: first_kernel(outer, *refs)

    held, strips = [ROWS_SHAPE] * 3, [STRIP_SHAPE] * 2
    *known, inside, outside, start, end = in_vmem(run(True), core, [tile, *tables], held + strips + [EDGE_SHAPE] * 2, "first_outer", 5)
    outer = exchange_x(start, end) + exchange_y(inside, outside)
    *known, inside, outside = in_vmem(run(False), core, [tile, *tables, *known], held + strips, "first_inner", 20, {5: 0, 6: 1, 7: 2})
    return known, outer, exchange_y(inside, outside)


def second_section(core, coef, following, east, outer, inner, tables):
    def run(outer):
        return lambda *refs: middle_kernel(outer, *refs)

    held, strips = [ROWS_SHAPE] * 2, [STRIP_SHAPE] * 2
    shared = [coef, following, east]
    ins = [*shared, *outer[2:], *tables, *outer[:2]]
    *known, inside, outside, start, end = in_vmem(run(True), core, ins, held + strips + [EDGE_SHAPE] * 2, "second_outer", 8, scratch=[STRIPS, SIDE])
    edges = exchange_x(start, end)
    ins = [*shared, *inner, *tables, *known, inside, outside]
    *known, inside, outside = in_vmem(run(False), core, ins, held + [STRIPS_SHAPE] * 2, "second_inner", 20, {9: 0, 10: 1}, [STRIPS])
    inside, outside, *edges = lax.optimization_barrier((inside, outside, *edges))
    return known, edges, exchange_y(inside, outside)


def advanced(core, following, east, edges, strips, scale):
    ins = [following, east, *strips, scale, *edges]
    return in_vmem(last_kernel, core, ins, [PIECES_SHAPE], "advanced", 8, scratch=[ALL_STRIPS, SIDE])[0]


def group_rows(full):
    return slice(REST, MODES) if full else slice(0, REST)


def repeat(count, body):
    lax.fori_loop(0, count, lambda i, _: (body(i), 0)[1], 0)


def pack_kernel(core_ref, state_ref, out_ref):
    row = 1 - core_ref[0]

    def body(s):
        out_ref[s] = state_ref[row, s]

    repeat(SLOTS, body)


def merge_kernel(core_ref, big_ref, state_ref, got_ref, out_ref):
    core = core_ref[0]

    def put(full):
        def body(block):
            out_ref[block, group_rows(full)] = state_ref[core, 0 : SLOTS if full else REST, block]
            out_ref[block, group_rows(not full)] = got_ref[0 : REST if full else SLOTS, block]

        repeat(BLOCKS, body)

    pl.when(core == big_ref[0])(lambda: put(True))
    pl.when(core != big_ref[0])(lambda: put(False))


def split_kernel(own, core_ref, big_ref, pieces_ref, out_ref):
    def get(full):
        slots = SLOTS if full else REST

        def body(block):
            out_ref[0:slots, block] = pieces_ref[block, group_rows(full)]
            if not full:
                out_ref[slots:SLOTS, block] = jnp.zeros((SLOTS - slots, HALVES, 128), F32)

        repeat(BLOCKS, body)

    for full in (False, True):
        pl.when((core_ref[0] == big_ref[0]) == (full == own))(lambda full=full: get(full))


def split_own_kernel(core_ref, big_ref, pieces_ref, out_ref, row, done):
    split_kernel(True, core_ref, big_ref, pieces_ref, row)
    copy = pltpu.make_async_copy(row, out_ref.at[core_ref[0]], done)
    copy.start()
    copy.wait()


def finish_kernel(core_ref, got_ref, _, out_ref, done):
    copy = pltpu.make_async_copy(got_ref, out_ref.at[1 - core_ref[0]], done)
    copy.start()
    copy.wait()


ROW = (SLOTS, BLOCKS, HALVES, 128)
ROW_SHAPE = jax.ShapeDtypeStruct(ROW, F32)
STATE_SHAPE = jax.ShapeDtypeStruct((2, *ROW), F32)
SLOTS_SHAPE = jax.ShapeDtypeStruct((BLOCKS, MODES, HALVES, 128), F32)


def moved(kernel, places, shape, name, aliases={}, scratch=()):
    spec = {"s": pl.BlockSpec(memory_space=pltpu.SMEM), "v": pl.BlockSpec(memory_space=pltpu.VMEM), "a": pl.BlockSpec(memory_space=pl.ANY)}
    return pl.pallas_call(
        kernel,
        in_specs=[spec[p] for p in places[:-1]],
        out_specs=spec[places[-1]],
        out_shape=shape,
        input_output_aliases=aliases,
        scratch_shapes=list(scratch),
        cost_estimate=pl.CostEstimate(flops=int(2e9), bytes_accessed=0, transcendentals=0),
        compiler_params=pltpu.CompilerParams(vmem_limit_bytes=LIMIT),
        name=name,
    )


def to_pieces(core, big, state):
    state = state.reshape(2, SLOTS, FIELDS, 2 * BLOCKS, 128).transpose(0, 1, 3, 2, 4).reshape(2, *ROW)
    got = lax.ppermute(moved(pack_kernel, "svv", ROW_SHAPE, "pack")(core, state), "mode", [(0, 1), (1, 0)])
    return moved(merge_kernel, "ssvvv", SLOTS_SHAPE, "merge")(core, big, state, got)


def from_pieces(core, big, pieces):
    got = lax.ppermute(moved(lambda *refs: split_kernel(False, *refs), "ssvv", ROW_SHAPE, "split_send")(core, big, pieces), "mode", [(0, 1), (1, 0)])
    semaphore = pltpu.SemaphoreType.DMA
    state = moved(split_own_kernel, "ssva", STATE_SHAPE, "split_own", scratch=[pltpu.VMEM(ROW, F32), semaphore])(core, big, pieces)
    state = moved(finish_kernel, "svaa", STATE_SHAPE, "finish", {2: 0}, [semaphore])(core, got, state)
    return state.reshape(2, SLOTS, 2 * BLOCKS, FIELDS, 128).transpose(0, 1, 3, 2, 4).reshape(2, SLOTS, FIELDS, BLOCKS * LANES)


def ring(size, step):
    return [(i, (i + step) % size) for i in range(size)]


def exchange_x(start, end):
    size = lax.axis_size("gx_hi")
    return lax.ppermute(end, "gx_hi", ring(size, 1)), lax.ppermute(start, "gx_hi", ring(size, -1))


def exchange_y(inside, outside):
    place = [(chip * 2 + side) * 2 + core for side in range(2) for chip in range(8) for core in range(2)]
    pairs = [(place[i], place[(i + 1) % 32]) for i in range(1, 32, 2)]
    swap = pairs + [(b, a) for a, b in pairs]
    return lax.ppermute(inside, "mode", [(0, 1), (1, 0)]), lax.ppermute(outside, ("gx_lo", "gy", "mode"), swap)


def shards(chaos_state, mode_group, mode_degrees):
    core = lax.axis_index("mode").astype(jnp.int32).reshape(1)
    evaluate, proj, scale, big = make_tables(mode_group, mode_degrees)
    tables = (evaluate, proj, lane_operators(), scale)
    pieces = to_pieces(core, big, chaos_state)
    tile = lax.all_to_all(pieces.reshape(XROWS, PIECE, 128), ("gx_lo", "mode"), 0, 0, tiled=True)
    (coef, east, following), outer, inner = first_section(core, tile, tables)
    (east, following), edges, strips = second_section(core, coef, following, east, outer, inner, tables)
    tile = advanced(core, following, east, edges, strips, scale)
    pieces = lax.all_to_all(tile, ("gx_lo", "mode"), 0, 0, tiled=True).reshape(SLOTS_SHAPE.shape)
    return from_pieces(core, big, pieces)


def solution(mesh):
    fine = Mesh(mesh.devices.reshape(4, 8, 2, 2), ("gx_hi", "gx_lo", "gy", "mode"))
    spec = P(("gx_hi", "gx_lo"), "mode", None, "gy")
    return jax.shard_map(shards, mesh=fine, in_specs=(spec, P(), P()), out_specs=spec, check_vma=False)
```
